256 devices in a mesh: illum: 4 (over x), gy: 16 (over y, z_lo, core), gx: 4 (over z_hi).
Axes of the slice: x: 4, y: 4, z: 8 (z_hi: 4, z_lo: 2; z = z_hi * 2 + z_lo), core: 2. Of those that a mesh axis runs over, the one named last changes fastest.
Arguments:
- incident: float32 [4, 2, 2048, 8192], P('illum', None, 'gy', 'gx'), may hold values from -6 to 6
- labels: int32 [2, 2048, 4, 4, 512], P(None, 'gy', 'gx', 'illum'), may hold values from 0 to 7
Outputs:
- exit_field: float32 [4, 2, 2048, 8192], P('illum', None, 'gy', 'gx')
- far_field: float32 [4, 2, 512, 512], P('illum', None, 'gy', 'gx')
The draws below stay inside these ranges and needn't reach their ends.
Inputs may be any that keep to these rules, and one draw needn't show every extreme that they name: Material labels index the tables.
All inputs are finite; a program needn't handle non-finite values.
Results may differ from the reference program's by a relative error of at most 0.0003.
Values may be sent and summed in bfloat16 or wider, within the bound.
A program may use at most 64 MiB of HBM per device.

```python
import math
import jax
import jax.numpy as jnp
from jax import lax

CY = 128
CX = 2048
SLICES = 2
SUB = 2
DET = 512
NY = 2048
NX = 8192
QX = 512
N_ILLUM = 4
N_GX = 4


def edge_profile(count, tile, reach):
    position = jnp.arange(count, dtype=jnp.int32) % tile
    distance = jnp.minimum(position, tile - 1 - position)
    inner = jnp.where(distance < reach, 1.0, 0.1)
    return jnp.where(distance == reach - 1, 2.5, inner).astype(jnp.float32)


def draw_incident(key, part):
    reach = 2 * SUB * SLICES
    rows_prof = edge_profile(NY, CY, reach)
    cols_prof = edge_profile(NX, CX, reach)
    profile = jnp.maximum(rows_prof[:, None], cols_prof[None, :])
    base = jax.random.normal(key, (N_ILLUM, 2, NY, NX), jnp.float32)
    return jnp.clip(base * profile[None, None], -6.0, 6.0).astype(jnp.float32)


def touch_ends(drawn, key, least, top_value):
    longest = drawn.shape.index(max(drawn.shape))
    spots = []
    for shift in (0, 1):
        where = [jax.random.randint(jax.random.fold_in(key, axis), (), 0, length) for axis, length in enumerate(drawn.shape)]
        where[longest] = (where[longest] + shift) % drawn.shape[longest]
        spots.append(tuple(where))
    return drawn.at[spots[0]].set(least).at[spots[1]].set(top_value)


def setup_inputs(seed: int = 0) -> dict:
    splits = jax.random.split(jax.random.key(seed), 3)
    incident = draw_incident(jax.random.fold_in(splits[2], 71), 0)
    labels = touch_ends(jax.random.randint(splits[1], (SLICES, NY, N_GX, N_ILLUM, QX), 0, 8), jax.random.fold_in(splits[1], 1), 0, 7).astype(jnp.int32)
    return {"incident": incident, "labels": labels}


PHASE = (0.0, 0.03125, 0.0625, 0.09375, 0.125, 0.15625, 0.1875, 0.25)
DAMP = (1.0, 0.99609375, 0.9921875, 0.98828125, 0.984375, 0.9765625, 0.96875, 0.9375)
RATE = 0.24

def laplace(field):
    padded = jnp.pad(field, 1)
    return padded[:-2, 1:-1] + padded[2:, 1:-1] + padded[1:-1, :-2] + padded[1:-1, 2:] - 4.0 * field

def advance(real, imag, phase, damp):
    real = damp * (real - (RATE * laplace(imag) + phase * imag))
    imag = damp * (imag + (RATE * laplace(real) + phase * real))
    return (real, imag)

def reference(incident, labels):
    grid_labels = labels.reshape(SLICES, NY, NX)
    phase_all = jnp.array(PHASE, jnp.float32)[grid_labels]
    damp_all = jnp.array(DAMP, jnp.float32)[grid_labels]
    rows_pos = jnp.arange(NY, dtype=jnp.int32)
    cols_pos = jnp.arange(NX, dtype=jnp.int32)
    freqs = jnp.arange(DET, dtype=jnp.int32) - DET // 2
    angle_y = jnp.mod(freqs[:, None] * rows_pos[None, :], NY).astype(jnp.float32) * (2.0 * math.pi / NY)
    angle_x = jnp.mod(cols_pos[:, None] * freqs[None, :], NX).astype(jnp.float32) * (2.0 * math.pi / NX)
    cos_y, sin_y = (jnp.cos(angle_y), jnp.sin(angle_y))
    cos_x, sin_x = (jnp.cos(angle_x), jnp.sin(angle_x))
    high = lax.Precision.HIGHEST
    scale = 1.0 / math.sqrt(NY * NX)
    exits = []
    fars = []
    for angle in range(N_ILLUM):
        real = incident[angle, 0]
        imag = incident[angle, 1]
        for slab in range(SLICES):
            phase = phase_all[slab]
            damp = damp_all[slab]

            def substep(step, state):
                return advance(state[0], state[1], phase, damp)
            real, imag = lax.fori_loop(0, SUB, substep, (real, imag))
        exits.append(jnp.stack([real, imag]))
        g_real = jnp.dot(real, cos_x, precision=high, preferred_element_type=jnp.float32) + jnp.dot(imag, sin_x, precision=high, preferred_element_type=jnp.float32)
        g_imag = jnp.dot(imag, cos_x, precision=high, preferred_element_type=jnp.float32) - jnp.dot(real, sin_x, precision=high, preferred_element_type=jnp.float32)
        f_real = jnp.dot(cos_y, g_real, precision=high, preferred_element_type=jnp.float32) + jnp.dot(sin_y, g_imag, precision=high, preferred_element_type=jnp.float32)
        f_imag = jnp.dot(cos_y, g_imag, precision=high, preferred_element_type=jnp.float32) - jnp.dot(sin_y, g_real, precision=high, preferred_element_type=jnp.float32)
        fars.append(jnp.stack([f_real, f_imag]) * scale)
    return (jnp.stack(exits), jnp.stack(fars))
```

```python
import functools
import math

import jax
import jax.numpy as jnp
import ml_dtypes
import numpy as np
from jax import lax
from jax.experimental import pallas as pl
from jax.experimental.pallas import tpu as pltpu
from jax.sharding import PartitionSpec as P

MESH = pl.DeviceIdType.MESH
SUB = 2
DET = 512
RATE = 0.24
PARTS = 1
F32 = jnp.float32
BF16 = jnp.bfloat16


def split(values):
    high = values.astype(ml_dtypes.bfloat16)
    low = (values - high.astype(np.float64)).astype(ml_dtypes.bfloat16)
    return np.stack([high, low])


def tables(det, cy, cx, ny, nx):
    cols = np.arange(cx)
    kappa = np.arange(det // 2) + 0.5
    angle = 2.0 * math.pi * cols[:, None] * kappa[None, :] / nx
    cos, sin = np.cos(angle), np.sin(angle)
    blocks = []
    for m in range(det // 256):
        blocks += [cos[:, 128 * m : 128 * m + 128], sin[:, 128 * m : 128 * m + 128]]
    wave_x = split(np.concatenate(blocks, axis=1))
    shift = math.pi * cols / nx
    turn = np.stack([np.cos(shift), np.sin(shift)]).astype(np.float32)
    turn = np.broadcast_to(turn.reshape(2, cx // 128, 1, 128), (2, cx // 128, 8, 128)).copy()
    ky = np.arange(det) - det // 2
    waves = []
    for tile in range(ny // cy):
        rows = tile * cy + np.arange(cy)
        angle = 2.0 * math.pi * ((ky[:, None] * rows[None, :]) % ny) / ny
        both = np.concatenate([np.cos(angle), np.sin(angle)], axis=1)
        waves.append(split(both / math.sqrt(ny * nx)))
    return wave_x, turn, np.stack(waves)


def lane_ids(rows):
    return lax.broadcasted_iota(jnp.int32, (rows, 128), 1)


def only_if(ok, value, other):
    flags = jnp.full(value.shape, ok.astype(jnp.int32), jnp.int32)
    return jnp.where(flags > 0, value, other)


def pack_edge(tiles, right):
    lane = lane_ids(8)
    out = jnp.zeros((8, 128), F32)
    for t in range(tiles.shape[0] // 8):
        piece = tiles[8 * t : 8 * t + 8]
        shift = (8 * t + (8 if right else 0)) % 128
        if shift:
            piece = pltpu.roll(piece, shift, 1)
        out = jnp.where(lane // 8 == t, piece, out)
    return out


def unpack_edges(left, right, t, fill, left_ok, right_ok):
    lane = lane_ids(8)
    shift_l, shift_r = (120 - 8 * t) % 128, (128 - 8 * t) % 128
    left = pltpu.roll(left, shift_l, 1) if shift_l else left
    right = pltpu.roll(right, shift_r, 1) if shift_r else right
    left = only_if(left_ok, left, fill)
    right = only_if(right_ok, right, fill)
    return jnp.where(lane < 8, right, jnp.where(lane >= 120, left, fill))


def coefficients(label):
    last = label > 6.5
    swing = jnp.where(last, 8.0, label) * (1.0 / (32.0 * RATE)) - 4.0
    loss = label + jnp.maximum(label - 4.0, 0.0) + jnp.where(last, 6.0, 0.0)
    damp = jnp.where(label < -0.5, 0.0, 1.0 - loss * (1.0 / 256.0))
    return swing, damp


def chunks_of(slices, cy, parts):
    if parts == 1:
        return [(s, 0, cy) for s in range(slices)]
    cut = cy // 2 + 16
    return [(s, a, b) for a, b in ((0, cut), (cut, cy)) for s in range(slices)]


def kernel(
    dims, inc, lab, wx_hbm, ey_hbm, turn, exit_ref, far_ref,
    lab_in, stage, out_stage, labs, edge_src, edges, rowbuf, pack_lab, pack_fld, colbuf, corner,
    fld, swing, damp, lhs, wx, ey, gsend, grecv, rhs, fsend, frecv,
    sem_in, sem_out, ag_send, ag_recv, edge_send, edge_recv, row_send, row_recv,
    col_send, col_recv, cl_send, cl_recv, cor_send, cor_recv, g_send, g_recv, f_send, f_recv,
):
    n_il, n_gy, n_gx = dims
    i, j, g = lax.axis_index("illum"), lax.axis_index("gy"), lax.axis_index("gx")
    slices, cy, qx = lab.shape
    cx = inc.shape[2]
    tiles = cx // 128
    per_q = qx // 128
    det = fsend.shape[0]
    parts = PARTS
    size = cy // parts

    def dev(illum=None, gy=None, gx=None):
        return (
            i if illum is None else illum,
            j if gy is None else gy,
            g if gx is None else gx,
        )

    def add(value, step, count):
        return lax.rem(value + (step + count), count)

    def remote(src, dst, send, recv, target):
        return pltpu.make_async_remote_copy(
            src_ref=src, dst_ref=dst, send_sem=send, recv_sem=recv,
            device_id=target, device_id_type=MESH,
        )

    load_lab = pltpu.make_async_copy(lab, lab_in, sem_in.at[0])
    load_fld = pltpu.make_async_copy(inc, stage, sem_in.at[1])
    load_wx = pltpu.make_async_copy(wx_hbm, wx, sem_in.at[2])
    load_ey = pltpu.make_async_copy(ey_hbm.at[j], ey, sem_in.at[3])
    load_lab.start()
    load_fld.start()

    barrier = pltpu.get_barrier_semaphore()
    peers = [dev(illum=add(i, d, n_il)) for d in range(1, n_il)]
    for step in (-1, 1):
        peers += [dev(illum=k, gy=add(j, step, n_gy)) for k in range(n_il)]
        peers += [dev(illum=k, gx=add(g, step, n_gx)) for k in range(n_il)]
    peers += [dev(gx=add(g, d, n_gx)) for d in range(2, n_gx - 1)]
    peers += [dev(gy=add(j, d, n_gy)) for d in range(2, n_gy - 1)]
    for peer in peers:
        pl.semaphore_signal(barrier, inc=1, device_id=peer, device_id_type=MESH)
    load_wx.start()
    load_ey.start()

    load_lab.wait()
    for s in range(slices):
        labs[i, s] = lab_in[s].astype(F32).astype(BF16)
    for e, top in ((0, 0), (1, cy - 8)):
        both = jnp.concatenate([lab_in[s, top : top + 8, :].astype(F32) for s in range(slices)])
        edge_src[e] = both.astype(BF16)
    for s in range(slices):
        pack_lab[0, s] = pack_edge(lab_in[s, :, 0:128].astype(F32), False)
        pack_lab[1, s] = pack_edge(lab_in[s, :, qx - 128 : qx].astype(F32), True)
    load_fld.wait()
    for f in range(2):
        pack_fld[0, f] = pack_edge(stage[f, :, 0:128], False)
        pack_fld[1, f] = pack_edge(stage[f, :, cx - 128 : cx], True)

    pl.semaphore_wait(barrier, len(peers))

    chunks = chunks_of(slices, cy, parts)
    il_next, il_prev = add(i, 1, n_il), add(i, -1, n_il)
    il_far = add(i, 2, n_il)

    def chunk_copy(n, way, second, quarter):
        s, a, b = chunks[n]
        mid = a + (b - a) // 32 * 16
        if second:
            a, b = (a, mid) if way == 0 else (mid, b)
        view = labs.at[quarter, s, pl.ds(a, b - a), :]
        slot = 2 * way + int(second)
        return remote(
            view, view, ag_send.at[n, slot], ag_recv.at[n, slot],
            dev(illum=il_next if way == 0 else il_prev),
        )

    pending = []

    def go(copy):
        copy.start()
        pending.append(copy)

    for way in range(2):
        go(chunk_copy(0, way, False, i))
    col_copies, cl_pairs = [], []
    for side, step in ((0, -1), (1, 1)):
        there = add(g, step, n_gx)
        go(remote(
            pack_fld.at[side], colbuf.at[1 - side, pl.ds(0, 2)], col_send.at[side], col_recv.at[side],
            dev(gx=there),
        ))
        @pl.when(i == (0 if side == 0 else n_il - 1))
        def _():
            for k in range(n_il):
                remote(
                    pack_lab.at[side], colbuf.at[1 - side, pl.ds(2, 2)],
                    cl_send.at[side, k], cl_recv.at[side], dev(illum=k, gx=there),
                ).start()
    for side, step in ((0, -1), (1, 1)):
        there = add(j, step, n_gy)
        src = stage.at[:, pl.ds(0 if side == 0 else cy - 8, 8), :]
        go(remote(src, rowbuf.at[1 - side], row_send.at[side], row_recv.at[side], dev(gy=there)))
        for d in range(n_il):
            go(remote(
                edge_src.at[side], edges.at[1 - side, i], edge_send.at[side, d], edge_recv.at[side, d],
                dev(illum=add(i, d, n_il), gy=there),
            ))
    for n in range(1, len(chunks)):
        for way in range(2):
            go(chunk_copy(n, way, False, i))

    for side in range(2):
        remote(pack_fld.at[side], colbuf.at[1 - side, pl.ds(0, 2)], col_send.at[side], col_recv.at[side], dev()).wait_recv()
        remote(pack_lab.at[side], colbuf.at[1 - side, pl.ds(2, 2)], cl_send.at[side, 0], cl_recv.at[side], dev()).wait_recv()
    for side, step in ((0, -1), (1, 1)):
        go(remote(
            colbuf, corner.at[1 - side], cor_send.at[side], cor_recv.at[side],
            dev(gy=add(j, step, n_gy)),
        ))

    def forward(n):
        for way in range(2):
            src = il_prev if way == 0 else il_next
            chunk_copy(n, way, False, src).wait_recv()
            go(chunk_copy(n, way, True, src))

    def arrived(n):
        for way in range(2):
            chunk_copy(n, way, True, il_far).wait_recv()

    up_ok, down_ok = j > 0, j < n_gy - 1
    left_ok, right_ok = g > 0, g < n_gx - 1

    def assemble_field(h):
        first = h * size
        for f in range(2):
            def main(c, carry):
                lanes = pl.ds(pl.multiple_of(c * 128, 128), 128)
                fld[f, c, 0:8, :] = jnp.zeros((8, 128), F32)
                fld[f, c, size + 24 : size + 32, :] = jnp.zeros((8, 128), F32)
                fld[f, c, 16 : size + 16, :] = stage[f, first : first + size, lanes]
                if h == 0:
                    fld[f, c, 8:16, :] = only_if(up_ok, rowbuf[0, f, :, lanes], 0.0)
                else:
                    fld[f, c, 8:16, :] = stage[f, first - 8 : first, lanes]
                if h == parts - 1:
                    fld[f, c, size + 16 : size + 24, :] = only_if(down_ok, rowbuf[1, f, :, lanes], 0.0)
                else:
                    fld[f, c, size + 16 : size + 24, :] = stage[f, first + size : first + size + 8, lanes]
                return carry

            lax.fori_loop(0, tiles, main, 0)
            fld[f, tiles, 0:8, :] = jnp.zeros((8, 128), F32)
            fld[f, tiles, size + 24 : size + 32, :] = jnp.zeros((8, 128), F32)

        def put(f, row, value):
            fld[f, tiles, row : row + 8, :] = value

        edge_tiles(h, (0, 1), 0.0, put)

    def edge_tiles(h, which, fill, put):
        total = cy // 8
        for w in which:
            left, right = colbuf[0, w], colbuf[1, w]
            for t in range(h * size // 8 - 1, (h + 1) * size // 8 + 1):
                row = 16 + 8 * t - h * size
                if t < 0:
                    value = unpack_edges(corner[0, 0, w], corner[0, 1, w], total - 1, fill, left_ok & up_ok, right_ok & up_ok)
                elif t >= total:
                    value = unpack_edges(corner[1, 0, w], corner[1, 1, w], 0, fill, left_ok & down_ok, right_ok & down_ok)
                else:
                    value = unpack_edges(left, right, t, fill, left_ok, right_ok)
                put(w, row, value)

    def set_coefs(c, row, rows, label):
        a, b = coefficients(label)
        swing[c, row : row + rows, :] = a
        damp[c, row : row + rows, :] = b

    def assemble_coefs(h, s):
        first = h * size

        def main(c, carry):
            q = c // per_q
            lanes = pl.ds(pl.multiple_of(lax.rem(c, per_q) * 128, 128), 128)
            set_coefs(c, 16, size, labs[q, s, first : first + size, lanes].astype(F32))
            if h == 0:
                top = only_if(up_ok, edges[0, q, :, lanes].astype(F32)[8 * s : 8 * s + 8], -1.0)
            else:
                top = labs[q, s, first - 16 : first, lanes].astype(F32)[8:16]
            set_coefs(c, 8, 8, top)
            if h == parts - 1:
                bottom = only_if(down_ok, edges[1, q, :, lanes].astype(F32)[8 * s : 8 * s + 8], -1.0)
            else:
                bottom = labs[q, s, first + size : first + size + 16, lanes].astype(F32)[0:8]
            set_coefs(c, size + 16, 8, bottom)
            return carry

        lax.fori_loop(0, tiles, main, 0)
        edge_tiles(h, (2 + s,), -1.0, lambda w, row, value: set_coefs(tiles, row, 8, value))

    def half_step(target, source, sign):
        lane = lane_ids(8)

        def column(c, carry):
            before = lax.rem(c + tiles, tiles + 1)
            after = lax.rem(c + 1, tiles + 1)
            for t in range(1, size // 8 + 3):
                r = 8 * t
                mid = fld[source, c, r : r + 8, :]
                vert = fld[source, c, r - 1 : r + 7, :] + fld[source, c, r + 1 : r + 9, :]
                left = pltpu.roll(jnp.where(lane == 127, fld[source, before, r : r + 8, :], mid), 1, 1)
                right = pltpu.roll(jnp.where(lane == 0, fld[source, after, r : r + 8, :], mid), 127, 1)
                total = vert + (left + right) + swing[c, r : r + 8, :] * mid
                fld[target, c, r : r + 8, :] = damp[c, r : r + 8, :] * (fld[target, c, r : r + 8, :] + (sign * RATE) * total)
            return carry

        lax.fori_loop(0, tiles + 1, column, 0)

    def transform(h):
        first = h * size

        def modulate(c, carry):
            lanes = pl.ds(pl.multiple_of(c * 128, 128), 128)
            cos = jnp.concatenate([turn[0, c]] * (size // 8))
            sin = jnp.concatenate([turn[1, c]] * (size // 8))
            real = fld[0, c, 16 : size + 16, :]
            imag = fld[1, c, 16 : size + 16, :]
            out_stage[0, first : first + size, lanes] = real
            out_stage[1, first : first + size, lanes] = imag
            for n, value in enumerate((real * cos - imag * sin, real * sin + imag * cos)):
                high = value.astype(BF16)
                lhs[0, n * size : (n + 1) * size, lanes] = high
                lhs[1, n * size : (n + 1) * size, lanes] = (value - high.astype(F32)).astype(BF16)
            return carry

        lax.fori_loop(0, tiles, modulate, 0)
        pltpu.make_async_copy(
            out_stage.at[:, pl.ds(first, size), :], exit_ref.at[:, pl.ds(first, size), :], sem_out.at[h]
        ).start()
        lane = lane_ids(8)
        for m in range(det // 256):
            cols = slice(256 * m, 256 * m + 256)
            prod = jnp.dot(lhs[0], wx[0, :, cols], preferred_element_type=F32)
            prod += jnp.dot(lhs[1], wx[0, :, cols], preferred_element_type=F32)
            prod += jnp.dot(lhs[0], wx[1, :, cols], preferred_element_type=F32)
            c_re, s_re = prod[:size, :128], prod[:size, 128:]
            c_im, s_im = prod[size:, :128], prod[size:, 128:]
            rank = 128 * m + lane
            for block, freq, g_re, g_im in (
                (n_gx // 2 + m, rank, c_re + s_im, c_im - s_re),
                (n_gx // 2 - 1 - m, -rank - 1, c_re - s_im, c_im + s_re),
            ):
                quarter = lax.rem((freq + det) * g, n_gx) * (4 // n_gx)
                f_re = jnp.where(quarter == 0, 1.0, jnp.where(quarter == 2, -1.0, 0.0))
                f_im = jnp.where(quarter == 1, -1.0, jnp.where(quarter == 3, 1.0, 0.0))
                f_re = jnp.concatenate([f_re] * (size // 8))
                f_im = jnp.concatenate([f_im] * (size // 8))
                gsend[block, first : first + size, 0:128] = g_re * f_re - g_im * f_im
                gsend[block, first : first + size, 128:256] = g_re * f_im + g_im * f_re

    def g_copy(h, d):
        rows = pl.ds(h * size, size)
        block = add(g, d, n_gx)
        return remote(
            gsend.at[block, rows, :], grecv.at[d - 1, rows, :],
            g_send.at[h, d - 1], g_recv.at[h, d - 1], dev(gx=block),
        )

    per_part = slices
    ready_rows = False
    for h in range(parts):
        for s in range(slices):
            n = h * per_part + s
            forward(n)
            if not ready_rows:
                for side in range(2):
                    remote(stage.at[:, pl.ds(0, 8), :], rowbuf.at[1 - side], row_send.at[side], row_recv.at[side], dev()).wait_recv()
                    for d in range(n_il):
                        remote(edge_src.at[side], edges.at[1 - side, i], edge_send.at[side, d], edge_recv.at[side, d], dev()).wait_recv()
                    remote(colbuf, corner.at[1 - side], cor_send.at[side], cor_recv.at[side], dev()).wait_recv()
                ready_rows = True
            if s == 0:
                assemble_field(h)
            arrived(n)
            assemble_coefs(h, s)

            def substep(step, carry):
                half_step(0, 1, -1.0)
                half_step(1, 0, 1.0)
                return carry

            lax.fori_loop(0, SUB, substep, 0)
        if h == 0:
            load_wx.wait()
        transform(h)
        for d in range(1, n_gx):
            go(g_copy(h, d))

    load_ey.wait()
    for h in range(parts):
        for d in range(1, n_gx):
            g_copy(h, d).wait_recv()
    total = gsend[g]
    for d in range(1, n_gx):
        total = total + grecv[d - 1]
    high = total.astype(BF16)
    low = (total - high.astype(F32)).astype(BF16)
    for n, value in enumerate((high, low)):
        rhs[n, 0:cy, :] = value
        rhs[n, cy : 2 * cy, 0:128] = value[:, 128:256]
        rhs[n, cy : 2 * cy, 128:256] = -value[:, 0:128]
    fsend[...] = (
        jnp.dot(ey[0], rhs[0], preferred_element_type=F32)
        + jnp.dot(ey[1], rhs[0], preferred_element_type=F32)
        + jnp.dot(ey[0], rhs[1], preferred_element_type=F32)
    )
    share = det // n_gy

    def f_copy(d):
        there = add(j, d, n_gy)
        return remote(
            fsend.at[pl.ds(pl.multiple_of(there * share, share), share), :], frecv.at[d - 1],
            f_send.at[d - 1], f_recv.at[d - 1], dev(gy=there),
        )

    for d in range(1, n_gy):
        go(f_copy(d))
    acc = fsend[pl.ds(pl.multiple_of(j * share, share), share), :]
    for d in range(1, n_gy):
        f_copy(d).wait_recv()
        acc = acc + frecv[d - 1]
    row_id = lax.broadcasted_iota(jnp.int32, (128, 128), 0)
    col_id = lax.broadcasted_iota(jnp.int32, (128, 128), 1)
    mirror = jnp.full((128, 128), (g < n_gx // 2).astype(jnp.int32), jnp.int32)
    order = jnp.where(jnp.where(mirror > 0, 127 - col_id, col_id) == row_id, 1.0, 0.0)
    for n in range(2):
        far_ref[n] = jnp.dot(
            acc[:, 128 * n : 128 * n + 128], order, precision=lax.Precision.HIGHEST, preferred_element_type=F32
        )

    for copy in pending:
        copy.wait_send()
    for side in range(2):
        @pl.when(i == (0 if side == 0 else n_il - 1))
        def _():
            for k in range(n_il):
                remote(pack_lab.at[side], colbuf.at[1 - side, pl.ds(2, 2)], cl_send.at[side, k], cl_recv.at[side], dev()).wait_send()
    for h in range(parts):
        rows = pl.ds(h * size, size)
        pltpu.make_async_copy(out_stage.at[:, rows, :], exit_ref.at[:, rows, :], sem_out.at[h]).wait()


def on_device(dims, det, incident, labels):
    n_il, n_gy, n_gx = dims
    slices, cy = labels.shape[:2]
    qx = labels.shape[4]
    cx = incident.shape[3]
    ny, nx = cy * n_gy, cx * n_gx
    wave_x, turn, wave_y = tables(det, cy, cx, ny, nx)
    tiles = cx // 128
    size = cy // PARTS
    share = det // n_gy
    n_chunks = len(chunks_of(slices, cy, PARTS))
    dma = pltpu.SemaphoreType.DMA
    vmem = pltpu.VMEM
    any_spec = pl.BlockSpec(memory_space=pl.ANY)
    vmem_spec = pl.BlockSpec(memory_space=pltpu.VMEM)
    field, far = pl.pallas_call(
        functools.partial(kernel, dims),
        out_shape=(
            jax.ShapeDtypeStruct((2, cy, cx), F32),
            jax.ShapeDtypeStruct((2, share, 128), F32),
        ),
        in_specs=[any_spec] * 4 + [vmem_spec],
        out_specs=(any_spec, vmem_spec),
        scratch_shapes=[
            vmem((slices, cy, qx), jnp.int32),
            vmem((2, cy, cx), F32),
            vmem((2, cy, cx), F32),
            vmem((n_il, slices, cy, qx), BF16),
            vmem((2, 8 * slices, qx), BF16),
            vmem((2, n_il, 8 * slices, qx), BF16),
            vmem((2, 2, 8, cx), F32),
            vmem((2, slices, 8, 128), F32),
            vmem((2, 2, 8, 128), F32),
            vmem((2, 2 + slices, 8, 128), F32),
            vmem((2, 2, 2 + slices, 8, 128), F32),
            vmem((2, tiles + 1, size + 32, 128), F32),
            vmem((tiles + 1, size + 32, 128), F32),
            vmem((tiles + 1, size + 32, 128), F32),
            vmem((2, 2 * size, cx), BF16),
            vmem((2, cx, det), BF16),
            vmem((2, det, 2 * cy), BF16),
            vmem((n_gx, cy, 256), F32),
            vmem((n_gx - 1, cy, 256), F32),
            vmem((2, 2 * cy, 256), BF16),
            vmem((det, 256), F32),
            vmem((n_gy - 1, share, 256), F32),
            dma((4,)),
            dma((PARTS,)),
            dma((n_chunks, 4)),
            dma((n_chunks, 4)),
            dma((2, n_il)),
            dma((2, n_il)),
            dma((2,)),
            dma((2,)),
            dma((2,)),
            dma((2,)),
            dma((2, n_il)),
            dma((2,)),
            dma((2,)),
            dma((2,)),
            dma((PARTS, n_gx - 1)),
            dma((PARTS, n_gx - 1)),
            dma((n_gy - 1,)),
            dma((n_gy - 1,)),
        ],
        compiler_params=pltpu.CompilerParams(
            collective_id=0, has_side_effects=True, vmem_limit_bytes=48 * 1024 * 1024
        ),
    )(
        incident.reshape(2, cy, cx),
        labels.reshape(slices, cy, qx),
        jnp.asarray(wave_x),
        jnp.asarray(wave_y),
        jnp.asarray(turn),
    )
    return field[None], far[None]


def solution(mesh, det=DET):
    dims = tuple(mesh.shape[name] for name in ("illum", "gy", "gx"))
    in_specs = (P("illum", None, "gy", "gx"), P(None, "gy", "gx", "illum", None))
    out_specs = (P("illum", None, "gy", "gx"), P("illum", None, "gy", "gx"))
    return jax.shard_map(
        functools.partial(on_device, dims, det), mesh=mesh, in_specs=in_specs, out_specs=out_specs, check_vma=False
    )
```

```python
import functools
import math

import jax
import jax.numpy as jnp
import ml_dtypes
import numpy as np
from jax import lax
from jax.experimental import pallas as pl
from jax.experimental.pallas import tpu as pltpu
from jax.sharding import PartitionSpec as P

MESH = pl.DeviceIdType.MESH
SUB = 2
DET = 512
RATE = 0.24
PARTS = 1
F32 = jnp.float32
BF16 = jnp.bfloat16


def split(values):
    high = values.astype(ml_dtypes.bfloat16)
    low = (values - high.astype(np.float64)).astype(ml_dtypes.bfloat16)
    return np.stack([high, low])


def tables(det, cy, cx, ny, nx):
    cols = np.arange(cx)
    kappa = np.arange(det // 2) + 0.5
    angle = 2.0 * math.pi * cols[:, None] * kappa[None, :] / nx
    cos, sin = np.cos(angle), np.sin(angle)
    blocks = []
    for m in range(det // 256):
        blocks += [cos[:, 128 * m : 128 * m + 128], sin[:, 128 * m : 128 * m + 128]]
    wave_x = split(np.concatenate(blocks, axis=1))
    shift = math.pi * cols / nx
    turn = np.stack([np.cos(shift), np.sin(shift)]).astype(np.float32)
    turn = np.broadcast_to(turn.reshape(2, cx // 128, 1, 128), (2, cx // 128, 8, 128)).copy()
    ky = np.arange(det) - det // 2
    waves = []
    for tile in range(ny // cy):
        rows = tile * cy + np.arange(cy)
        angle = 2.0 * math.pi * ((ky[:, None] * rows[None, :]) % ny) / ny
        both = np.concatenate([np.cos(angle), np.sin(angle)], axis=1)
        waves.append(split(both / math.sqrt(ny * nx)))
    return wave_x, turn, np.stack(waves)


def lane_ids(rows):
    return lax.broadcasted_iota(jnp.int32, (rows, 128), 1)


def only_if(ok, value, other):
    flags = jnp.full(value.shape, ok.astype(jnp.int32), jnp.int32)
    return jnp.where(flags > 0, value, other)


def pack_edge(tiles, right):
    lane = lane_ids(8)
    out = jnp.zeros((8, 128), F32)
    for t in range(tiles.shape[0] // 8):
        piece = tiles[8 * t : 8 * t + 8]
        shift = (8 * t + (8 if right else 0)) % 128
        if shift:
            piece = pltpu.roll(piece, shift, 1)
        out = jnp.where(lane // 8 == t, piece, out)
    return out


def unpack_edges(left, right, t, fill, left_ok, right_ok):
    lane = lane_ids(8)
    shift_l, shift_r = (120 - 8 * t) % 128, (128 - 8 * t) % 128
    left = pltpu.roll(left, shift_l, 1) if shift_l else left
    right = pltpu.roll(right, shift_r, 1) if shift_r else right
    left = only_if(left_ok, left, fill)
    right = only_if(right_ok, right, fill)
    return jnp.where(lane < 8, right, jnp.where(lane >= 120, left, fill))


def coefficients(label):
    last = label > 6.5
    swing = jnp.where(last, 8.0, label) * (1.0 / (32.0 * RATE)) - 4.0
    loss = label + jnp.maximum(label - 4.0, 0.0) + jnp.where(last, 6.0, 0.0)
    damp = jnp.where(label < -0.5, 0.0, 1.0 - loss * (1.0 / 256.0))
    return swing, damp


def chunks_of(slices, cy, parts):
    if parts == 1:
        return [(s, 0, cy) for s in range(slices)]
    cut = cy // 2 + 16
    return [(s, a, b) for a, b in ((0, cut), (cut, cy)) for s in range(slices)]


def kernel(
    dims, inc, lab, wx_hbm, ey_hbm, turn, exit_ref, far_ref,
    lab_in, stage, out_stage, labs, edge_src, edges, rowbuf, pack_lab, pack_fld, colbuf, corner,
    fld_re, fld_im, swing, damp, lhs, wx, ey, gsend, grecv, rhs, fsend, frecv,
    sem_in, sem_out, ag_send, ag_recv, edge_send, edge_recv, row_send, row_recv,
    col_send, col_recv, cl_send, cl_recv, cor_send, cor_recv, g_send, g_recv, f_send, f_recv,
):
    n_il, n_gy, n_gx = dims
    fld = (fld_re, fld_im)
    i, j, g = lax.axis_index("illum"), lax.axis_index("gy"), lax.axis_index("gx")
    slices, cy, qx = lab.shape
    cx = inc.shape[2]
    tiles = cx // 128
    per_q = qx // 128
    det = fsend.shape[0]
    parts = PARTS
    size = cy // parts

    def dev(illum=None, gy=None, gx=None):
        return (
            i if illum is None else illum,
            j if gy is None else gy,
            g if gx is None else gx,
        )

    def add(value, step, count):
        return lax.rem(value + (step + count), count)

    def remote(src, dst, send, recv, target):
        return pltpu.make_async_remote_copy(
            src_ref=src, dst_ref=dst, send_sem=send, recv_sem=recv,
            device_id=target, device_id_type=MESH,
        )

    load_lab = pltpu.make_async_copy(lab, lab_in, sem_in.at[0])
    load_fld = pltpu.make_async_copy(inc, stage, sem_in.at[1])
    load_wx = pltpu.make_async_copy(wx_hbm, wx, sem_in.at[2])
    load_ey = pltpu.make_async_copy(ey_hbm.at[j], ey, sem_in.at[3])
    load_lab.start()
    load_fld.start()

    barrier = pltpu.get_barrier_semaphore()
    peers = [dev(illum=add(i, d, n_il)) for d in range(1, n_il)]
    for step in (-1, 1):
        peers += [dev(illum=k, gy=add(j, step, n_gy)) for k in range(n_il)]
        peers += [dev(illum=k, gx=add(g, step, n_gx)) for k in range(n_il)]
    peers += [dev(gx=add(g, d, n_gx)) for d in range(2, n_gx - 1)]
    peers += [dev(gy=add(j, d, n_gy)) for d in range(2, n_gy - 1)]
    for peer in peers:
        pl.semaphore_signal(barrier, inc=1, device_id=peer, device_id_type=MESH)
    load_wx.start()
    load_ey.start()

    load_lab.wait()
    for s in range(slices):
        labs[i, s] = lab_in[s].astype(F32).astype(BF16)
    for e, top in ((0, 0), (1, cy - 8)):
        both = jnp.concatenate([lab_in[s, top : top + 8, :].astype(F32) for s in range(slices)])
        edge_src[e] = both.astype(BF16)
    for s in range(slices):
        pack_lab[0, s] = pack_edge(lab_in[s, :, 0:128].astype(F32), False)
        pack_lab[1, s] = pack_edge(lab_in[s, :, qx - 128 : qx].astype(F32), True)
    load_fld.wait()
    for f in range(2):
        pack_fld[0, f] = pack_edge(stage[f, :, 0:128], False)
        pack_fld[1, f] = pack_edge(stage[f, :, cx - 128 : cx], True)

    pl.semaphore_wait(barrier, len(peers))

    chunks = chunks_of(slices, cy, parts)
    il_next, il_prev = add(i, 1, n_il), add(i, -1, n_il)
    il_far = add(i, 2, n_il)

    def chunk_copy(n, way, second, quarter):
        s, a, b = chunks[n]
        mid = a + (b - a) // 32 * 16
        if second:
            a, b = (a, mid) if way == 0 else (mid, b)
        view = labs.at[quarter, s, pl.ds(a, b - a), :]
        slot = 2 * way + int(second)
        return remote(
            view, view, ag_send.at[n, slot], ag_recv.at[n, slot],
            dev(illum=il_next if way == 0 else il_prev),
        )

    pending = []

    def go(copy):
        copy.start()
        pending.append(copy)

    for way in range(2):
        go(chunk_copy(0, way, False, i))
    col_copies, cl_pairs = [], []
    for side, step in ((0, -1), (1, 1)):
        there = add(g, step, n_gx)
        go(remote(
            pack_fld.at[side], colbuf.at[1 - side, pl.ds(0, 2)], col_send.at[side], col_recv.at[side],
            dev(gx=there),
        ))
        @pl.when(i == (0 if side == 0 else n_il - 1))
        def _():
            for k in range(n_il):
                remote(
                    pack_lab.at[side], colbuf.at[1 - side, pl.ds(2, 2)],
                    cl_send.at[side, k], cl_recv.at[side], dev(illum=k, gx=there),
                ).start()
    for side, step in ((0, -1), (1, 1)):
        there = add(j, step, n_gy)
        src = stage.at[:, pl.ds(0 if side == 0 else cy - 8, 8), :]
        go(remote(src, rowbuf.at[1 - side], row_send.at[side], row_recv.at[side], dev(gy=there)))
        for d in range(n_il):
            go(remote(
                edge_src.at[side], edges.at[1 - side, i], edge_send.at[side, d], edge_recv.at[side, d],
                dev(illum=add(i, d, n_il), gy=there),
            ))
    for n in range(1, len(chunks)):
        for way in range(2):
            go(chunk_copy(n, way, False, i))

    for side in range(2):
        remote(pack_fld.at[side], colbuf.at[1 - side, pl.ds(0, 2)], col_send.at[side], col_recv.at[side], dev()).wait_recv()
        remote(pack_lab.at[side], colbuf.at[1 - side, pl.ds(2, 2)], cl_send.at[side, 0], cl_recv.at[side], dev()).wait_recv()
    for side, step in ((0, -1), (1, 1)):
        go(remote(
            colbuf, corner.at[1 - side], cor_send.at[side], cor_recv.at[side],
            dev(gy=add(j, step, n_gy)),
        ))

    def forward(n):
        for way in range(2):
            src = il_prev if way == 0 else il_next
            chunk_copy(n, way, False, src).wait_recv()
            go(chunk_copy(n, way, True, src))

    def arrived(n):
        for way in range(2):
            chunk_copy(n, way, True, il_far).wait_recv()

    up_ok, down_ok = j > 0, j < n_gy - 1
    left_ok, right_ok = g > 0, g < n_gx - 1

    def assemble_field(h):
        first = h * size
        for f in range(2):
            def main(c, carry):
                lanes = pl.ds(pl.multiple_of(c * 128, 128), 128)
                fld[f][c, 0:8, :] = jnp.zeros((8, 128), F32)
                fld[f][c, size + 24 : size + 32, :] = jnp.zeros((8, 128), F32)
                fld[f][c, 16 : size + 16, :] = stage[f, first : first + size, lanes]
                if h == 0:
                    fld[f][c, 8:16, :] = only_if(up_ok, rowbuf[0, f, :, lanes], 0.0)
                else:
                    fld[f][c, 8:16, :] = stage[f, first - 8 : first, lanes]
                if h == parts - 1:
                    fld[f][c, size + 16 : size + 24, :] = only_if(down_ok, rowbuf[1, f, :, lanes], 0.0)
                else:
                    fld[f][c, size + 16 : size + 24, :] = stage[f, first + size : first + size + 8, lanes]
                return carry

            lax.fori_loop(0, tiles, main, 0)
            fld[f][tiles, 0:8, :] = jnp.zeros((8, 128), F32)
            fld[f][tiles, size + 24 : size + 32, :] = jnp.zeros((8, 128), F32)

        def put(f, row, value):
            fld[f][tiles, row : row + 8, :] = value

        edge_tiles(h, (0, 1), 0.0, put)

    def edge_tiles(h, which, fill, put):
        total = cy // 8
        for w in which:
            left, right = colbuf[0, w], colbuf[1, w]
            for t in range(h * size // 8 - 1, (h + 1) * size // 8 + 1):
                row = 16 + 8 * t - h * size
                if t < 0:
                    value = unpack_edges(corner[0, 0, w], corner[0, 1, w], total - 1, fill, left_ok & up_ok, right_ok & up_ok)
                elif t >= total:
                    value = unpack_edges(corner[1, 0, w], corner[1, 1, w], 0, fill, left_ok & down_ok, right_ok & down_ok)
                else:
                    value = unpack_edges(left, right, t, fill, left_ok, right_ok)
                put(w, row, value)

    def set_coefs(c, row, rows, label):
        a, b = coefficients(label)
        swing[c, row : row + rows, :] = a
        damp[c, row : row + rows, :] = b

    def assemble_coefs(h, s):
        first = h * size

        def main(c, carry):
            q = c // per_q
            lanes = pl.ds(pl.multiple_of(lax.rem(c, per_q) * 128, 128), 128)
            set_coefs(c, 16, size, labs[q, s, first : first + size, lanes].astype(F32))
            if h == 0:
                top = only_if(up_ok, edges[0, q, :, lanes].astype(F32)[8 * s : 8 * s + 8], -1.0)
            else:
                top = labs[q, s, first - 16 : first, lanes].astype(F32)[8:16]
            set_coefs(c, 8, 8, top)
            if h == parts - 1:
                bottom = only_if(down_ok, edges[1, q, :, lanes].astype(F32)[8 * s : 8 * s + 8], -1.0)
            else:
                bottom = labs[q, s, first + size : first + size + 16, lanes].astype(F32)[0:8]
            set_coefs(c, size + 16, 8, bottom)
            return carry

        lax.fori_loop(0, tiles, main, 0)
        edge_tiles(h, (2 + s,), -1.0, lambda w, row, value: set_coefs(tiles, row, 8, value))

    def half_step(target, source, sign):
        rows = size + 16
        lane = lane_ids(rows)

        def column(c):
            before = (c + tiles) % (tiles + 1)
            after = (c + 1) % (tiles + 1)
            mid = source[c, 8 : 8 + rows, :]
            vert = source[c, 7 : 7 + rows, :] + source[c, 9 : 9 + rows, :]
            left = pltpu.roll(jnp.where(lane == 127, source[before, 8 : 8 + rows, :], mid), 1, 1)
            right = pltpu.roll(jnp.where(lane == 0, source[after, 8 : 8 + rows, :], mid), 127, 1)
            total = vert + (left + right) + swing[c, 8 : 8 + rows, :] * mid
            target[c, 8 : 8 + rows, :] = damp[c, 8 : 8 + rows, :] * (target[c, 8 : 8 + rows, :] + (sign * RATE) * total)

        for c in range(tiles + 1):
            column(c)

    def transform(h):
        first = h * size

        def modulate(c, carry):
            lanes = pl.ds(pl.multiple_of(c * 128, 128), 128)
            cos = jnp.concatenate([turn[0, c]] * (size // 8))
            sin = jnp.concatenate([turn[1, c]] * (size // 8))
            real = fld[0][c, 16 : size + 16, :]
            imag = fld[1][c, 16 : size + 16, :]
            out_stage[0, first : first + size, lanes] = real
            out_stage[1, first : first + size, lanes] = imag
            for n, value in enumerate((real * cos - imag * sin, real * sin + imag * cos)):
                high = value.astype(BF16)
                lhs[0, n * size : (n + 1) * size, lanes] = high
                lhs[1, n * size : (n + 1) * size, lanes] = (value - high.astype(F32)).astype(BF16)
            return carry

        lax.fori_loop(0, tiles, modulate, 0)
        pltpu.make_async_copy(
            out_stage.at[:, pl.ds(first, size), :], exit_ref.at[:, pl.ds(first, size), :], sem_out.at[h]
        ).start()
        lane = lane_ids(8)
        for m in range(det // 256):
            cols = slice(256 * m, 256 * m + 256)
            prod = jnp.dot(lhs[0], wx[0, :, cols], preferred_element_type=F32)
            prod += jnp.dot(lhs[1], wx[0, :, cols], preferred_element_type=F32)
            prod += jnp.dot(lhs[0], wx[1, :, cols], preferred_element_type=F32)
            c_re, s_re = prod[:size, :128], prod[:size, 128:]
            c_im, s_im = prod[size:, :128], prod[size:, 128:]
            rank = 128 * m + lane
            for block, freq, g_re, g_im in (
                (n_gx // 2 + m, rank, c_re + s_im, c_im - s_re),
                (n_gx // 2 - 1 - m, -rank - 1, c_re - s_im, c_im + s_re),
            ):
                quarter = lax.rem((freq + det) * g, n_gx) * (4 // n_gx)
                f_re = jnp.where(quarter == 0, 1.0, jnp.where(quarter == 2, -1.0, 0.0))
                f_im = jnp.where(quarter == 1, -1.0, jnp.where(quarter == 3, 1.0, 0.0))
                f_re = jnp.concatenate([f_re] * (size // 8))
                f_im = jnp.concatenate([f_im] * (size // 8))
                gsend[block, first : first + size, 0:128] = g_re * f_re - g_im * f_im
                gsend[block, first : first + size, 128:256] = g_re * f_im + g_im * f_re

    def g_copy(h, d):
        rows = pl.ds(h * size, size)
        block = add(g, d, n_gx)
        return remote(
            gsend.at[block, rows, :], grecv.at[d - 1, rows, :],
            g_send.at[h, d - 1], g_recv.at[h, d - 1], dev(gx=block),
        )

    per_part = slices
    ready_rows = False
    for h in range(parts):
        for s in range(slices):
            n = h * per_part + s
            forward(n)
            if not ready_rows:
                for side in range(2):
                    remote(stage.at[:, pl.ds(0, 8), :], rowbuf.at[1 - side], row_send.at[side], row_recv.at[side], dev()).wait_recv()
                    for d in range(n_il):
                        remote(edge_src.at[side], edges.at[1 - side, i], edge_send.at[side, d], edge_recv.at[side, d], dev()).wait_recv()
                    remote(colbuf, corner.at[1 - side], cor_send.at[side], cor_recv.at[side], dev()).wait_recv()
                ready_rows = True
            if s == 0:
                assemble_field(h)
            arrived(n)
            assemble_coefs(h, s)

            def substep(step, carry):
                half_step(fld[0], fld[1], -1.0)
                half_step(fld[1], fld[0], 1.0)
                return carry

            lax.fori_loop(0, SUB, substep, 0)
        if h == 0:
            load_wx.wait()
        transform(h)
        for d in range(1, n_gx):
            go(g_copy(h, d))

    load_ey.wait()
    for h in range(parts):
        for d in range(1, n_gx):
            g_copy(h, d).wait_recv()
    total = gsend[g]
    for d in range(1, n_gx):
        total = total + grecv[d - 1]
    high = total.astype(BF16)
    low = (total - high.astype(F32)).astype(BF16)
    for n, value in enumerate((high, low)):
        rhs[n, 0:cy, :] = value
        rhs[n, cy : 2 * cy, 0:128] = value[:, 128:256]
        rhs[n, cy : 2 * cy, 128:256] = -value[:, 0:128]
    fsend[...] = (
        jnp.dot(ey[0], rhs[0], preferred_element_type=F32)
        + jnp.dot(ey[1], rhs[0], preferred_element_type=F32)
        + jnp.dot(ey[0], rhs[1], preferred_element_type=F32)
    )
    share = det // n_gy

    def f_copy(d):
        there = add(j, d, n_gy)
        return remote(
            fsend.at[pl.ds(pl.multiple_of(there * share, share), share), :], frecv.at[d - 1],
            f_send.at[d - 1], f_recv.at[d - 1], dev(gy=there),
        )

    for d in range(1, n_gy):
        go(f_copy(d))
    acc = fsend[pl.ds(pl.multiple_of(j * share, share), share), :]
    for d in range(1, n_gy):
        f_copy(d).wait_recv()
        acc = acc + frecv[d - 1]
    row_id = lax.broadcasted_iota(jnp.int32, (128, 128), 0)
    col_id = lax.broadcasted_iota(jnp.int32, (128, 128), 1)
    mirror = jnp.full((128, 128), (g < n_gx // 2).astype(jnp.int32), jnp.int32)
    order = jnp.where(jnp.where(mirror > 0, 127 - col_id, col_id) == row_id, 1.0, 0.0)
    for n in range(2):
        far_ref[n] = jnp.dot(
            acc[:, 128 * n : 128 * n + 128], order, precision=lax.Precision.HIGHEST, preferred_element_type=F32
        )

    for copy in pending:
        copy.wait_send()
    for side in range(2):
        @pl.when(i == (0 if side == 0 else n_il - 1))
        def _():
            for k in range(n_il):
                remote(pack_lab.at[side], colbuf.at[1 - side, pl.ds(2, 2)], cl_send.at[side, k], cl_recv.at[side], dev()).wait_send()
    for h in range(parts):
        rows = pl.ds(h * size, size)
        pltpu.make_async_copy(out_stage.at[:, rows, :], exit_ref.at[:, rows, :], sem_out.at[h]).wait()


def on_device(dims, det, incident, labels):
    n_il, n_gy, n_gx = dims
    slices, cy = labels.shape[:2]
    qx = labels.shape[4]
    cx = incident.shape[3]
    ny, nx = cy * n_gy, cx * n_gx
    wave_x, turn, wave_y = tables(det, cy, cx, ny, nx)
    tiles = cx // 128
    size = cy // PARTS
    share = det // n_gy
    n_chunks = len(chunks_of(slices, cy, PARTS))
    dma = pltpu.SemaphoreType.DMA
    vmem = pltpu.VMEM
    any_spec = pl.BlockSpec(memory_space=pl.ANY)
    vmem_spec = pl.BlockSpec(memory_space=pltpu.VMEM)
    field, far = pl.pallas_call(
        functools.partial(kernel, dims),
        out_shape=(
            jax.ShapeDtypeStruct((2, cy, cx), F32),
            jax.ShapeDtypeStruct((2, share, 128), F32),
        ),
        in_specs=[any_spec] * 4 + [vmem_spec],
        out_specs=(any_spec, vmem_spec),
        scratch_shapes=[
            vmem((slices, cy, qx), jnp.int32),
            vmem((2, cy, cx), F32),
            vmem((2, cy, cx), F32),
            vmem((n_il, slices, cy, qx), BF16),
            vmem((2, 8 * slices, qx), BF16),
            vmem((2, n_il, 8 * slices, qx), BF16),
            vmem((2, 2, 8, cx), F32),
            vmem((2, slices, 8, 128), F32),
            vmem((2, 2, 8, 128), F32),
            vmem((2, 2 + slices, 8, 128), F32),
            vmem((2, 2, 2 + slices, 8, 128), F32),
            vmem((tiles + 1, size + 32, 128), F32),
            vmem((tiles + 1, size + 32, 128), F32),
            vmem((tiles + 1, size + 32, 128), F32),
            vmem((tiles + 1, size + 32, 128), F32),
            vmem((2, 2 * size, cx), BF16),
            vmem((2, cx, det), BF16),
            vmem((2, det, 2 * cy), BF16),
            vmem((n_gx, cy, 256), F32),
            vmem((n_gx - 1, cy, 256), F32),
            vmem((2, 2 * cy, 256), BF16),
            vmem((det, 256), F32),
            vmem((n_gy - 1, share, 256), F32),
            dma((4,)),
            dma((PARTS,)),
            dma((n_chunks, 4)),
            dma((n_chunks, 4)),
            dma((2, n_il)),
            dma((2, n_il)),
            dma((2,)),
            dma((2,)),
            dma((2,)),
            dma((2,)),
            dma((2, n_il)),
            dma((2,)),
            dma((2,)),
            dma((2,)),
            dma((PARTS, n_gx - 1)),
            dma((PARTS, n_gx - 1)),
            dma((n_gy - 1,)),
            dma((n_gy - 1,)),
        ],
        compiler_params=pltpu.CompilerParams(
            collective_id=0, has_side_effects=True, vmem_limit_bytes=48 * 1024 * 1024
        ),
    )(
        incident.reshape(2, cy, cx),
        labels.reshape(slices, cy, qx),
        jnp.asarray(wave_x),
        jnp.asarray(wave_y),
        jnp.asarray(turn),
    )
    return field[None], far[None]


def solution(mesh, det=DET):
    dims = tuple(mesh.shape[name] for name in ("illum", "gy", "gx"))
    in_specs = (P("illum", None, "gy", "gx"), P(None, "gy", "gx", "illum", None))
    out_specs = (P("illum", None, "gy", "gx"), P("illum", None, "gy", "gx"))
    return jax.shard_map(
        functools.partial(on_device, dims, det), mesh=mesh, in_specs=in_specs, out_specs=out_specs, check_vma=False
    )
```

```python
import functools
import math

import jax
import jax.numpy as jnp
import ml_dtypes
import numpy as np
from jax import lax
from jax.experimental import pallas as pl
from jax.experimental.pallas import tpu as pltpu
from jax.sharding import PartitionSpec as P

MESH = pl.DeviceIdType.MESH
SUB = 2
DET = 512
RATE = 0.24
PARTS = 1
F32 = jnp.float32
BF16 = jnp.bfloat16


def split(values):
    high = values.astype(ml_dtypes.bfloat16)
    low = (values - high.astype(np.float64)).astype(ml_dtypes.bfloat16)
    return np.stack([high, low])


def tables(det, cy, cx, ny, nx):
    cols = np.arange(cx)
    kappa = np.arange(det // 2) + 0.5
    angle = 2.0 * math.pi * cols[:, None] * kappa[None, :] / nx
    cos, sin = np.cos(angle), np.sin(angle)
    blocks = []
    for m in range(det // 256):
        blocks += [cos[:, 128 * m : 128 * m + 128], sin[:, 128 * m : 128 * m + 128]]
    wave_x = split(np.concatenate(blocks, axis=1))
    shift = math.pi * cols / nx
    turn = np.stack([np.cos(shift), np.sin(shift)]).astype(np.float32)
    turn = np.broadcast_to(turn.reshape(2, cx // 128, 1, 128), (2, cx // 128, 8, 128)).copy()
    share = det // (ny // cy)
    ky = (np.arange(det) - det // 2).reshape(-1, 2, share).transpose(1, 0, 2).reshape(-1)
    waves = []
    for tile in range(ny // cy):
        rows = tile * cy + np.arange(cy)
        angle = 2.0 * math.pi * ((ky[:, None] * rows[None, :]) % ny) / ny
        both = np.concatenate([np.cos(angle), np.sin(angle)], axis=1)
        waves.append(split(both / math.sqrt(ny * nx)))
    return wave_x, turn, np.stack(waves)


def lane_ids(rows):
    return lax.broadcasted_iota(jnp.int32, (rows, 128), 1)


def only_if(ok, value, other):
    flags = jnp.full(value.shape, ok.astype(jnp.int32), jnp.int32)
    return jnp.where(flags > 0, value, other)


def pack_edge(tiles, right):
    lane = lane_ids(8)
    out = jnp.zeros((8, 128), F32)
    for t in range(tiles.shape[0] // 8):
        piece = tiles[8 * t : 8 * t + 8]
        shift = (8 * t + (8 if right else 0)) % 128
        if shift:
            piece = pltpu.roll(piece, shift, 1)
        out = jnp.where(lane // 8 == t, piece, out)
    return out


def unpack_edges(left, right, t, fill, left_ok, right_ok):
    lane = lane_ids(8)
    shift_l, shift_r = (120 - 8 * t) % 128, (128 - 8 * t) % 128
    left = pltpu.roll(left, shift_l, 1) if shift_l else left
    right = pltpu.roll(right, shift_r, 1) if shift_r else right
    left = only_if(left_ok, left, fill)
    right = only_if(right_ok, right, fill)
    return jnp.where(lane < 8, right, jnp.where(lane >= 120, left, fill))


def coefficients(label):
    last = label > 6.5
    swing = jnp.where(last, 8.0, label) * (1.0 / (32.0 * RATE)) - 4.0
    loss = label + jnp.maximum(label - 4.0, 0.0) + jnp.where(last, 6.0, 0.0)
    damp = jnp.where(label < -0.5, 0.0, 1.0 - loss * (1.0 / 256.0))
    return swing, damp


def chunks_of(slices, cy, parts):
    if parts == 1:
        return [(s, 0, cy) for s in range(slices)]
    cut = cy // 2 + 16
    return [(s, a, b) for a, b in ((0, cut), (cut, cy)) for s in range(slices)]


def middle(n, a, b):
    step = (b - a) // 32 * 16
    return b - step if n % 2 else a + step


def kernel(
    dims, inc, lab, wx_hbm, ey_hbm, turn_hbm, exit_ref, far_ref,
    lab_in, stage, out_stage, labs, edge_src, pack_lab, ext, rowbuf, pack_fld, colbuf,
    fld_re, fld_im, swing, damp, turn, lhs, wx, ey, gown, gsend, grecv, rhs, fsend, fpair, fhalf, frecv,
    sem_lab, sem_in, sem_out, ag_send, ag_recv, edge_send, edge_recv, cl_send, cl_recv, ext_send, ext_recv,
    row_send, row_recv, col_send, col_recv, g_send, g_recv, pair_sem, f_send, f_recv,
):
    n_il, n_gy, n_gx = dims
    fld = (fld_re, fld_im)
    i, j, g = lax.axis_index("illum"), lax.axis_index("gy"), lax.axis_index("gx")
    _, slices, cy, qx = labs.shape
    cx = inc.shape[2]
    tiles = cx // 128
    per_q = qx // 128
    det = wx.shape[2]
    parts = PARTS
    size = cy // parts

    def dev(illum=None, gy=None, gx=None):
        return (
            i if illum is None else illum,
            j if gy is None else gy,
            g if gx is None else gx,
        )

    def add(value, step, count):
        return lax.rem(value + (step + count), count)

    def remote(src, dst, send, recv, target):
        return pltpu.make_async_remote_copy(
            src_ref=src, dst_ref=dst, send_sem=send, recv_sem=recv,
            device_id=target, device_id_type=MESH,
        )

    lab_rows = cy * per_q
    load_lab = [
        pltpu.make_async_copy(
            lab.at[pl.ds(s * lab_rows, lab_rows), :], lab_in.at[pl.ds(s * lab_rows, lab_rows), :], sem_lab.at[s]
        )
        for s in range(slices)
    ]
    load_fld = pltpu.make_async_copy(inc, stage, sem_in.at[1])
    load_wx = pltpu.make_async_copy(wx_hbm, wx, sem_in.at[2])
    load_ey = pltpu.make_async_copy(ey_hbm.at[j], ey, sem_in.at[3])
    load_turn = pltpu.make_async_copy(turn_hbm, turn, sem_in.at[4])
    for load in load_lab:
        load.start()
    load_fld.start()
    ext[i, 32:48, :] = jnp.zeros((16, qx), BF16)

    barrier = pltpu.get_barrier_semaphore()
    peers = [dev(illum=add(i, d, n_il)) for d in range(1, n_il)]
    peers += [
        dev(gy=add(j, dj, n_gy), gx=add(g, dg, n_gx))
        for dj in (-1, 0, 1) for dg in (-1, 0, 1) if dj or dg
    ]
    peers += [dev(gx=add(g, d, n_gx)) for d in range(2, n_gx - 1)]
    peers += [dev(gy=add(j, d, n_gy)) for d in range(2, n_gy, 2)]
    for peer in peers:
        pl.semaphore_signal(barrier, inc=1, device_id=peer, device_id_type=MESH)
    load_turn.start()
    load_wx.start()
    load_ey.start()

    def label_tile(s, row, rows, tile):
        return lab_in[pl.ds((s * cy + row) * per_q + tile, rows, stride=per_q), :].astype(F32)

    def own_labels(s):
        load_lab[s].wait()
        for tile in range(per_q):
            labs[i, s, :, 128 * tile : 128 * tile + 128] = label_tile(s, 0, cy, tile).astype(BF16)

    def label_edges():
        for e, top in ((0, 0), (1, cy - 8)):
            for tile in range(per_q):
                both = jnp.concatenate([label_tile(s, top, 8, tile) for s in range(slices)])
                edge_src[e, :, 128 * tile : 128 * tile + 128] = both.astype(BF16)
        for side, tile in ((0, 0), (1, per_q - 1)):
            both = jnp.concatenate([pack_edge(label_tile(s, 0, cy, tile), side == 1) for s in range(slices)])
            pack_lab[side] = both.astype(BF16)

    chunks = chunks_of(slices, cy, parts)
    il_next, il_prev = add(i, 1, n_il), add(i, -1, n_il)
    il_far = add(i, 2, n_il)

    def chunk_copy(n, way, kind, quarter):
        s, a, b = chunks[n]
        mid = middle(n, a, b)
        a, b = (a, mid) if (way == 0) == (kind != 1) else (mid, b)
        view = labs.at[quarter, s, pl.ds(a, b - a), :]
        slot = 3 * way + kind
        return remote(
            view, view, ag_send.at[n, slot], ag_recv.at[n, slot],
            dev(illum=il_next if way == 0 else il_prev),
        )

    pending = []

    def go(copy):
        copy.start()
        pending.append(copy)

    def start_chunk(copy):
        copy.start()

    def edge_copy(side):
        return remote(
            edge_src.at[side], ext.at[i, pl.ds(16 * (1 - side), 16), :], edge_send.at[side], edge_recv.at[side],
            dev(gy=add(j, 2 * side - 1, n_gy)),
        )

    def lab_col_copy(side, slot):
        return remote(
            pack_lab.at[side], ext.at[i, pl.ds(32, 16), pl.ds(128 * slot, 128)],
            cl_send.at[slot], cl_recv.at[slot], dev(gy=add(j, 1 - slot, n_gy), gx=add(g, 2 * side - 1, n_gx)),
        )

    def ext_copy(d):
        return remote(
            ext.at[i], ext.at[i], ext_send.at[d - 1], ext_recv.at[d - 1], dev(illum=add(i, d, n_il)),
        )

    def row_copy(side):
        src = inc.at[:, pl.ds(0 if side == 0 else cy - 8, 8), :]
        return remote(
            src, rowbuf.at[1 - side], row_send.at[side], row_recv.at[side], dev(gy=add(j, 2 * side - 1, n_gy))
        )

    def col_copy(side, slot):
        return remote(
            pack_fld.at[side], colbuf.at[1 - side, slot], col_send.at[side, slot], col_recv.at[side, slot],
            dev(gy=add(j, 1 - slot, n_gy), gx=add(g, 2 * side - 1, n_gx)),
        )

    def send_own(n):
        for kind in range(2):
            for way in range(2):
                start_chunk(chunk_copy(n, way, kind, i))

    def forward(n):
        for way in range(2):
            src = il_prev if way == 0 else il_next
            chunk_copy(n, way, 0, src).wait_recv()
            start_chunk(chunk_copy(n, way, 2, src))

    def arrived(n):
        for way in range(2):
            chunk_copy(n, way, 2, il_far).wait_recv()

    def near(n):
        for way in range(2):
            chunk_copy(n, way, 1, il_prev if way == 0 else il_next).wait_recv()

    up_ok, down_ok = j > 0, j < n_gy - 1
    left_ok, right_ok = g > 0, g < n_gx - 1

    def assemble_field(h):
        first = h * size
        for f in range(2):
            def main(c, carry):
                lanes = pl.ds(pl.multiple_of(c * 128, 128), 128)
                fld[f][c, 0:8, :] = jnp.zeros((8, 128), F32)
                fld[f][c, size + 24 : size + 32, :] = jnp.zeros((8, 128), F32)
                fld[f][c, 16 : size + 16, :] = stage[f, first : first + size, lanes]
                if h == 0:
                    fld[f][c, 8:16, :] = only_if(up_ok, rowbuf[0, f, :, lanes], 0.0)
                else:
                    fld[f][c, 8:16, :] = stage[f, first - 8 : first, lanes]
                if h == parts - 1:
                    fld[f][c, size + 16 : size + 24, :] = only_if(down_ok, rowbuf[1, f, :, lanes], 0.0)
                else:
                    fld[f][c, size + 16 : size + 24, :] = stage[f, first + size : first + size + 8, lanes]
                return carry

            lax.fori_loop(0, tiles, main, 0)
            fld[f][tiles, 0:8, :] = jnp.zeros((8, 128), F32)
            fld[f][tiles, size + 24 : size + 32, :] = jnp.zeros((8, 128), F32)

        def put(f, row, value):
            fld[f][tiles, row : row + 8, :] = value

        for f in range(2):
            edge_tiles(
                h, 0.0, lambda side, slot: colbuf[side, slot, f], lambda row, value: put(f, row, value)
            )

    def edge_tiles(h, fill, get, put):
        total = cy // 8
        for t in range(h * size // 8 - 1, (h + 1) * size // 8 + 1):
            slot, rank, ok = (0, total - 1, up_ok) if t < 0 else (2, 0, down_ok) if t >= total else (1, t, None)
            both = (left_ok, right_ok) if ok is None else (left_ok & ok, right_ok & ok)
            value = unpack_edges(get(0, slot), get(1, slot), rank, fill, *both)
            put(16 + 8 * t - h * size, value)

    def set_coefs(s, c, row, rows, label):
        a, b = coefficients(label)
        swing[s, c, row : row + rows, :] = a
        damp[s, c, row : row + rows, :] = b

    def quarter_coefs(s, q):
        def main(tile, carry):
            lanes = pl.ds(pl.multiple_of(tile * 128, 128), 128)
            set_coefs(s, q * per_q + tile, 16, cy, labs[q, s, :, lanes].astype(F32))
            return carry

        lax.fori_loop(0, per_q, main, 0)

    def halo_coefs(s):
        def main(c, carry):
            q = c // per_q
            lanes = pl.ds(pl.multiple_of(lax.rem(c, per_q) * 128, 128), 128)
            for row, first, ok in ((8, 0, up_ok), (cy + 16, 16, down_ok)):
                label = ext[q, first : first + 16, lanes].astype(F32)[8 * s : 8 * s + 8]
                set_coefs(s, c, row, 8, only_if(ok, label, -1.0))
            return carry

        lax.fori_loop(0, tiles, main, 0)

        def get(side, slot):
            both = ext[n_il - 1 if side == 0 else 0, 32:48, 128 * slot : 128 * slot + 128].astype(F32)
            return both[8 * s : 8 * s + 8]

        edge_tiles(0, -1.0, get, lambda row, value: set_coefs(s, tiles, row, 8, value))

    def half_step(s, target, source, sign):
        rows = (size + 16) // 2
        lane = lane_ids(rows)
        for part in range(2):
            r = 8 + rows * part
            before, mid = source[tiles, r : r + rows, :], source[0, r : r + rows, :]
            for c in range(tiles + 1):
                after = source[(c + 1) % (tiles + 1), r : r + rows, :]
                vert = source[c, r - 1 : r - 1 + rows, :] + source[c, r + 1 : r + 1 + rows, :]
                left = pltpu.roll(jnp.where(lane == 127, before, mid), 1, 1)
                right = pltpu.roll(jnp.where(lane == 0, after, mid), 127, 1)
                total = vert + (left + right) + swing[s, c, r : r + rows, :] * mid
                target[c, r : r + rows, :] = damp[s, c, r : r + rows, :] * (target[c, r : r + rows, :] + (sign * RATE) * total)
                before, mid = mid, after

    def transform(h):
        first = h * size

        def modulate(c, carry):
            lanes = pl.ds(pl.multiple_of(c * 128, 128), 128)
            cos = jnp.concatenate([turn[0, c]] * (size // 8))
            sin = jnp.concatenate([turn[1, c]] * (size // 8))
            real = fld[0][c, 16 : size + 16, :]
            imag = fld[1][c, 16 : size + 16, :]
            out_stage[0, first : first + size, lanes] = real
            out_stage[1, first : first + size, lanes] = imag
            for n, value in enumerate((real * cos - imag * sin, real * sin + imag * cos)):
                high = value.astype(BF16)
                lhs[0, n * size : (n + 1) * size, lanes] = high
                lhs[1, n * size : (n + 1) * size, lanes] = (value - high.astype(F32)).astype(BF16)
            return carry

        lax.fori_loop(0, tiles, modulate, 0)
        pltpu.make_async_copy(
            out_stage.at[:, pl.ds(first, size), :], exit_ref.at[:, pl.ds(first, size), :], sem_out.at[h]
        ).start()
        lane = lane_ids(8)
        for m in range(det // 256):
            cols = slice(256 * m, 256 * m + 256)
            prod = jnp.dot(lhs[0], wx[0, :, cols], preferred_element_type=F32)
            prod += jnp.dot(lhs[1], wx[0, :, cols], preferred_element_type=F32)
            prod += jnp.dot(lhs[0], wx[1, :, cols], preferred_element_type=F32)
            c_re, s_re = prod[:size, :128], prod[:size, 128:]
            c_im, s_im = prod[size:, :128], prod[size:, 128:]
            rank = 128 * m + lane
            for block, freq, g_re, g_im in (
                (n_gx // 2 + m, rank, c_re + s_im, c_im - s_re),
                (n_gx // 2 - 1 - m, -rank - 1, c_re - s_im, c_im + s_re),
            ):
                quarter = lax.rem((freq + det) * g, n_gx) * (4 // n_gx)
                f_re = jnp.where(quarter == 0, 1.0, jnp.where(quarter == 2, -1.0, 0.0))
                f_im = jnp.where(quarter == 1, -1.0, jnp.where(quarter == 3, 1.0, 0.0))
                f_re = jnp.concatenate([f_re] * (size // 8))
                f_im = jnp.concatenate([f_im] * (size // 8))
                value = jnp.concatenate([g_re * f_re - g_im * f_im, g_re * f_im + g_im * f_re], axis=1)
                gown[block, first : first + size, :] = value
                top = jnp.maximum(jnp.max(jnp.abs(value), axis=0, keepdims=True), 2.0**-110)
                level = jnp.ceil(jnp.log2(top) * 128.0)
                gsend[block, h, 0:16, :] = jnp.broadcast_to(level, (16, 256)).astype(jnp.int32).astype(jnp.int16)
                gsend[block, h, 16 : 16 + size, :] = (
                    jnp.round(value * (jnp.exp2(level * (-1.0 / 128.0)) * 32000.0)).astype(jnp.int32).astype(jnp.int16)
                )

            for block in (n_gx // 2 + m, n_gx // 2 - 1 - m):
                @pl.when(g != block)
                def _():
                    g_copy(h, lax.rem(block - g + n_gx, n_gx)).start()

    def g_copy(h, d):
        block = add(g, d, n_gx)
        return remote(
            gsend.at[block, h], grecv.at[d - 1, h], g_send.at[h, d - 1], g_recv.at[h, d - 1], dev(gx=block)
        )

    def g_total(h):
        total = gown[g, h * size : (h + 1) * size, :]
        for d in range(1, n_gx):
            g_copy(h, d).wait_recv()
            level = grecv[d - 1, h, 0:16, :].astype(jnp.int32).astype(F32)[0:1]
            unit = jnp.exp2(level * (1.0 / 128.0)) * (1.0 / 32000.0)
            total = total + grecv[d - 1, h, 16 : 16 + size, :].astype(jnp.int32).astype(F32) * unit
        return total

    own_labels(0)
    pl.semaphore_wait(barrier, len(peers))
    send_own(0)
    own_labels(1)
    label_edges()
    for side, owner in ((0, 0), (1, n_il - 1)):
        @pl.when(i == owner)
        def _():
            for slot in range(3):
                lab_col_copy(side, slot).start()
    for side in range(2):
        go(edge_copy(side))
    for side in range(2):
        go(row_copy(side))
    load_fld.wait()
    for f in range(2):
        pack_fld[0, f] = pack_edge(stage[f, :, 0:128], False)
        pack_fld[1, f] = pack_edge(stage[f, :, cx - 128 : cx], True)
    for side in range(2):
        for slot in range(3):
            go(col_copy(side, slot))
    forward(0)
    for side in range(2):
        edge_copy(side).wait_recv()
    @pl.when((i == 0) | (i == n_il - 1))
    def _():
        for slot in range(3):
            lab_col_copy(0, slot).wait_recv()
    for d in range(1, n_il):
        go(ext_copy(d))
    send_own(1)
    quarter_coefs(0, i)
    quarter_coefs(1, i)
    near(0)
    quarter_coefs(0, il_prev)
    quarter_coefs(0, il_next)
    for side in range(2):
        row_copy(side).wait_recv()
        for slot in range(3):
            col_copy(side, slot).wait_recv()
    assemble_field(0)
    for d in range(1, n_il):
        ext_copy(d).wait_recv()
    for s in range(slices):
        halo_coefs(s)
    arrived(0)
    quarter_coefs(0, il_far)
    for s in range(slices):
        def substep(step, carry):
            if s == 0:
                @pl.when(step == 1)
                def _():
                    forward(1)

            half_step(s, fld[0], fld[1], -1.0)
            half_step(s, fld[1], fld[0], 1.0)
            return carry

        lax.fori_loop(0, SUB, substep, 0)
        if s == 0:
            near(1)
            quarter_coefs(1, il_prev)
            quarter_coefs(1, il_next)
            arrived(1)
            quarter_coefs(1, il_far)
    load_turn.wait()
    load_wx.wait()
    transform(0)

    load_ey.wait()
    for h in range(parts):
        total = g_total(h)
        high = total.astype(BF16)
        low = (total - high.astype(F32)).astype(BF16)
        rows = slice(h * size, (h + 1) * size)
        for n, value in enumerate((high, low)):
            rhs[n, rows, :] = value
            rhs[n, cy + h * size : cy + (h + 1) * size, 0:128] = value[:, 128:256]
            rhs[n, cy + h * size : cy + (h + 1) * size, 128:256] = -value[:, 0:128]

    share = det // n_gy
    half = det // 2
    odd = lax.rem(j, 2)

    def wave_rows(parity):
        rows = pl.ds(pl.multiple_of(parity * half, half), half)
        return (
            jnp.dot(ey[0, rows, :], rhs[0], preferred_element_type=F32)
            + jnp.dot(ey[1, rows, :], rhs[0], preferred_element_type=F32)
            + jnp.dot(ey[0, rows, :], rhs[1], preferred_element_type=F32)
        )

    fsend[...] = wave_rows(1 - odd)
    pair = remote(fsend, fpair, pair_sem.at[0], pair_sem.at[1], dev(gy=j + 1 - 2 * odd))
    go(pair)
    own = wave_rows(odd)
    pair.wait_recv()
    fhalf[...] = own + fpair[...]

    def f_copy(d):
        there = add(j, d, n_gy)
        return remote(
            fhalf.at[pl.ds(pl.multiple_of(there // 2 * share, share), share), :], frecv.at[d // 2 - 1],
            f_send.at[d // 2 - 1], f_recv.at[d // 2 - 1], dev(gy=there),
        )

    for d in range(2, n_gy, 2):
        go(f_copy(d))
    acc = fhalf[pl.ds(pl.multiple_of(j // 2 * share, share), share), :]
    for d in range(2, n_gy, 2):
        f_copy(d).wait_recv()
        acc = acc + frecv[d // 2 - 1]
    row_id = lax.broadcasted_iota(jnp.int32, (128, 128), 0)
    col_id = lax.broadcasted_iota(jnp.int32, (128, 128), 1)
    mirror = jnp.full((128, 128), (g < n_gx // 2).astype(jnp.int32), jnp.int32)
    order = jnp.where(jnp.where(mirror > 0, 127 - col_id, col_id) == row_id, 1.0, 0.0)
    for n in range(2):
        far_ref[n] = jnp.dot(
            acc[:, 128 * n : 128 * n + 128], order, precision=lax.Precision.HIGHEST, preferred_element_type=F32
        )

    for copy in pending:
        copy.wait_send()
    for n in range(len(chunks)):
        for way in range(2):
            for kind in range(3):
                chunk_copy(n, way, kind, i).wait_send()
    for h in range(parts):
        for d in range(1, n_gx):
            g_copy(h, d).wait_send()
    @pl.when((i == 0) | (i == n_il - 1))
    def _():
        for slot in range(3):
            lab_col_copy(0, slot).wait_send()
    for h in range(parts):
        rows = pl.ds(h * size, size)
        pltpu.make_async_copy(out_stage.at[:, rows, :], exit_ref.at[:, rows, :], sem_out.at[h]).wait()


def on_device(dims, det, incident, labels):
    n_il, n_gy, n_gx = dims
    slices, cy = labels.shape[:2]
    hbm_spec = pl.BlockSpec(memory_space=pltpu.HBM)
    qx = labels.shape[4]
    cx = incident.shape[3]
    ny, nx = cy * n_gy, cx * n_gx
    wave_x, turn, wave_y = tables(det, cy, cx, ny, nx)
    tiles = cx // 128
    size = cy // PARTS
    share = det // n_gy
    n_chunks = len(chunks_of(slices, cy, PARTS))
    dma = pltpu.SemaphoreType.DMA
    vmem = pltpu.VMEM
    any_spec = pl.BlockSpec(memory_space=pl.ANY)
    vmem_spec = pl.BlockSpec(memory_space=pltpu.VMEM)
    field, far = pl.pallas_call(
        functools.partial(kernel, dims),
        out_shape=(
            pltpu.VMEM((2, cy, cx), F32),
            pltpu.VMEM((2, share, 128), F32),
        ),
        in_specs=[hbm_spec] * 5,
        out_specs=(any_spec, vmem_spec),
        scratch_shapes=[
            vmem((slices * cy * qx // 128, 128), jnp.int32),
            vmem((2, cy, cx), F32),
            vmem((2, cy, cx), F32),
            vmem((n_il, slices, cy, qx), BF16),
            vmem((2, 8 * slices, qx), BF16),
            vmem((2, 8 * slices, 128), BF16),
            vmem((n_il, 24 * slices, qx), BF16),
            vmem((2, 2, 8, cx), F32),
            vmem((2, 2, 8, 128), F32),
            vmem((2, 3, 2, 8, 128), F32),
            vmem((tiles + 1, size + 32, 128), F32),
            vmem((tiles + 1, size + 32, 128), F32),
            vmem((slices, tiles + 1, size + 32, 128), F32),
            vmem((slices, tiles + 1, size + 32, 128), F32),
            vmem((2, tiles, 8, 128), F32),
            vmem((2, 2 * size, cx), BF16),
            vmem((2, cx, det), BF16),
            vmem((2, det, 2 * cy), BF16),
            vmem((n_gx, cy, 256), F32),
            vmem((n_gx, PARTS, 16 + size, 256), jnp.int16),
            vmem((n_gx - 1, PARTS, 16 + size, 256), jnp.int16),
            vmem((2, 2 * cy, 256), BF16),
            vmem((det // 2, 256), F32),
            vmem((det // 2, 256), F32),
            vmem((det // 2, 256), F32),
            vmem((n_gy // 2 - 1, share, 256), F32),
            dma((slices,)),
            dma((5,)),
            dma((PARTS,)),
            dma((n_chunks, 6)),
            dma((n_chunks, 6)),
            dma((2,)),
            dma((2,)),
            dma((3,)),
            dma((3,)),
            dma((n_il - 1,)),
            dma((n_il - 1,)),
            dma((2,)),
            dma((2,)),
            dma((2, 3)),
            dma((2, 3)),
            dma((PARTS, n_gx - 1)),
            dma((PARTS, n_gx - 1)),
            dma((2,)),
            dma((n_gy // 2 - 1,)),
            dma((n_gy // 2 - 1,)),
        ],
        compiler_params=pltpu.CompilerParams(
            collective_id=0, has_side_effects=True, vmem_limit_bytes=48 * 1024 * 1024
        ),
    )(
        *(
            pltpu.with_memory_space_constraint(x, pltpu.HBM)
            for x in (
                incident.reshape(2, cy, cx),
                labels.reshape(slices * cy * qx // 128, 128),
                jnp.asarray(wave_x),
                jnp.asarray(wave_y),
                jnp.asarray(turn),
            )
        )
    )
    return field[None], far[None]


def solution(mesh, det=DET):
    dims = tuple(mesh.shape[name] for name in ("illum", "gy", "gx"))
    in_specs = (P("illum", None, "gy", "gx"), P(None, "gy", "gx", "illum", None))
    out_specs = (P("illum", None, "gy", "gx"), P("illum", None, "gy", "gx"))
    return jax.shard_map(
        functools.partial(on_device, dims, det), mesh=mesh, in_specs=in_specs, out_specs=out_specs, check_vma=False
    )
```

```python
import functools
import math

import jax
import jax.numpy as jnp
import ml_dtypes
import numpy as np
from jax import lax
from jax.experimental import pallas as pl
from jax.experimental.pallas import tpu as pltpu
from jax.sharding import PartitionSpec as P

MESH = pl.DeviceIdType.MESH
SUB = 2
DET = 512
RATE = 0.24
PARTS = 1
F32 = jnp.float32
BF16 = jnp.bfloat16


def split(values):
    high = values.astype(ml_dtypes.bfloat16)
    low = (values - high.astype(np.float64)).astype(ml_dtypes.bfloat16)
    return np.stack([high, low])


def tables(det, cy, cx, ny, nx):
    cols = np.arange(cx)
    kappa = np.arange(det // 2) + 0.5
    angle = 2.0 * math.pi * cols[:, None] * kappa[None, :] / nx
    cos, sin = np.cos(angle), np.sin(angle)
    blocks = []
    for m in range(det // 256):
        blocks += [cos[:, 128 * m : 128 * m + 128], sin[:, 128 * m : 128 * m + 128]]
    wave_x = split(np.concatenate(blocks, axis=1))
    shift = math.pi * cols / nx
    turn = np.stack([np.cos(shift), np.sin(shift)]).astype(np.float32)
    turn = np.broadcast_to(turn.reshape(2, cx // 128, 1, 128), (2, cx // 128, 8, 128)).copy()
    share = det // (ny // cy)
    ky = (np.arange(det) - det // 2).reshape(-1, 2, share).transpose(1, 0, 2).reshape(-1)
    waves = []
    for tile in range(ny // cy):
        rows = tile * cy + np.arange(cy)
        angle = 2.0 * math.pi * ((ky[:, None] * rows[None, :]) % ny) / ny
        both = np.concatenate([np.cos(angle), np.sin(angle)], axis=1)
        waves.append(split(both / math.sqrt(ny * nx)))
    return wave_x, turn, np.stack(waves)


def lane_ids(rows):
    return lax.broadcasted_iota(jnp.int32, (rows, 128), 1)


def only_if(ok, value, other):
    flags = jnp.full(value.shape, ok.astype(jnp.int32), jnp.int32)
    return jnp.where(flags > 0, value, other)


def pack_edge(tiles, right):
    lane = lane_ids(8)
    out = jnp.zeros((8, 128), F32)
    for t in range(tiles.shape[0] // 8):
        piece = tiles[8 * t : 8 * t + 8]
        shift = (8 * t + (8 if right else 0)) % 128
        if shift:
            piece = pltpu.roll(piece, shift, 1)
        out = jnp.where(lane // 8 == t, piece, out)
    return out


def unpack_edges(left, right, t, fill, left_ok, right_ok):
    lane = lane_ids(8)
    shift_l, shift_r = (120 - 8 * t) % 128, (128 - 8 * t) % 128
    left = pltpu.roll(left, shift_l, 1) if shift_l else left
    right = pltpu.roll(right, shift_r, 1) if shift_r else right
    left = only_if(left_ok, left, fill)
    right = only_if(right_ok, right, fill)
    return jnp.where(lane < 8, right, jnp.where(lane >= 120, left, fill))


def coefficients(label):
    last = label > 6.5
    swing = jnp.where(last, 8.0, label) * (1.0 / (32.0 * RATE)) - 4.0
    loss = label + jnp.maximum(label - 4.0, 0.0) + jnp.where(last, 6.0, 0.0)
    damp = jnp.where(label < -0.5, 0.0, 1.0 - loss * (1.0 / 256.0))
    return swing, damp


def encode(real, imag):
    levels, bodies = [], []
    for value in (real, imag):
        top = jnp.maximum(jnp.max(jnp.abs(value), axis=0, keepdims=True), 2.0**-110)
        level = jnp.ceil(jnp.log2(top) * 128.0)
        levels.append(level)
        bodies.append(jnp.round(value * (jnp.exp2(level * (-1.0 / 128.0)) * 32000.0)).astype(jnp.int32).astype(jnp.int16))
    row = lax.broadcasted_iota(jnp.int32, (16, 128), 0)
    shape = (16, 128)
    head = jnp.where(row == 0, jnp.broadcast_to(levels[0], shape), jnp.broadcast_to(levels[1], shape))
    return head.astype(jnp.int32).astype(jnp.int16), bodies[0], bodies[1]


def decode(block, rows):
    unit = jnp.exp2(block[0:16].astype(jnp.int32).astype(F32) * (1.0 / 128.0)) * (1.0 / 32000.0)
    return [
        block[16 + n * rows : 16 + (n + 1) * rows].astype(jnp.int32).astype(F32) * unit[n : n + 1] for n in range(2)
    ]


def chunks_of(slices, cy, parts):
    if parts == 1:
        return [(s, 0, cy) for s in range(slices)]
    cut = cy // 2 + 16
    return [(s, a, b) for a, b in ((0, cut), (cut, cy)) for s in range(slices)]


def middle(n, a, b):
    step = (b - a) // 32 * 16
    return b - step if n % 2 else a + step


def kernel(
    dims, inc, lab, wx_hbm, ey_hbm, turn_hbm, exit_ref, far_ref,
    lab_in, stage, out_stage, labs, edge_src, pack_lab, ext, rowbuf, pack_fld, colbuf,
    fld_re, fld_im, swing, damp, turn, lhs, wx, ey, gown, gsend, grecv, rhs, fsend, fpair, fhalf, fcode, frecv,
    sem_lab, sem_in, sem_out, ag_send, ag_recv, edge_send, edge_recv, cl_send, cl_recv, ext_send, ext_recv, extc_send, extc_recv,
    row_send, row_recv, col_send, col_recv, g_send, g_recv, pair_send, pair_recv, f_send, f_recv,
):
    n_il, n_gy, n_gx = dims
    fld = (fld_re, fld_im)
    i, j, g = lax.axis_index("illum"), lax.axis_index("gy"), lax.axis_index("gx")
    _, slices, cy, qx = labs.shape
    cx = inc.shape[2]
    tiles = cx // 128
    per_q = qx // 128
    det = wx.shape[2]
    parts = PARTS
    size = cy // parts

    def dev(illum=None, gy=None, gx=None):
        return (
            i if illum is None else illum,
            j if gy is None else gy,
            g if gx is None else gx,
        )

    def add(value, step, count):
        return lax.rem(value + (step + count), count)

    def remote(src, dst, send, recv, target):
        return pltpu.make_async_remote_copy(
            src_ref=src, dst_ref=dst, send_sem=send, recv_sem=recv,
            device_id=target, device_id_type=MESH,
        )

    lab_rows = cy * per_q
    load_lab = [
        pltpu.make_async_copy(
            lab.at[pl.ds(s * lab_rows, lab_rows), :], lab_in.at[pl.ds(s * lab_rows, lab_rows), :], sem_lab.at[s]
        )
        for s in range(slices)
    ]
    load_fld = pltpu.make_async_copy(inc, stage, sem_in.at[1])
    load_wx = pltpu.make_async_copy(wx_hbm, wx, sem_in.at[2])
    load_ey = pltpu.make_async_copy(ey_hbm.at[j], ey, sem_in.at[3])
    load_turn = pltpu.make_async_copy(turn_hbm, turn, sem_in.at[4])
    for load in load_lab:
        load.start()
    load_fld.start()

    barrier = pltpu.get_barrier_semaphore()
    peers = [dev(illum=add(i, d, n_il)) for d in range(1, n_il)]
    peers += [
        dev(gy=add(j, dj, n_gy), gx=add(g, dg, n_gx))
        for dj in (-1, 0, 1) for dg in (-1, 0, 1) if dj or dg
    ]
    peers += [dev(gx=add(g, d, n_gx)) for d in range(2, n_gx - 1)]
    peers += [dev(gy=add(j, d, n_gy)) for d in range(2, n_gy, 2)]
    for peer in peers:
        pl.semaphore_signal(barrier, inc=1, device_id=peer, device_id_type=MESH)
    load_turn.start()
    load_wx.start()
    load_ey.start()

    def label_tile(s, row, rows, tile):
        return lab_in[pl.ds((s * cy + row) * per_q + tile, rows, stride=per_q), :].astype(F32)

    def own_labels(s):
        load_lab[s].wait()
        for tile in range(per_q):
            labs[i, s, :, 128 * tile : 128 * tile + 128] = label_tile(s, 0, cy, tile).astype(BF16)

    def label_edges():
        for e, top in ((0, 0), (1, cy - 8)):
            for tile in range(per_q):
                both = jnp.concatenate([label_tile(s, top, 8, tile) for s in range(slices)])
                edge_src[e, :, 128 * tile : 128 * tile + 128] = both.astype(BF16)
        for side, tile in ((0, 0), (1, per_q - 1)):
            both = jnp.concatenate([pack_edge(label_tile(s, 0, cy, tile), side == 1) for s in range(slices)])
            pack_lab[side] = both.astype(BF16)

    chunks = chunks_of(slices, cy, parts)
    il_next, il_prev = add(i, 1, n_il), add(i, -1, n_il)
    il_far = add(i, 2, n_il)

    def chunk_copy(n, way, kind, quarter):
        s, a, b = chunks[n]
        mid = middle(n, a, b)
        a, b = (a, mid) if (way == 0) == (kind != 1) else (mid, b)
        view = labs.at[quarter, s, pl.ds(a, b - a), :]
        slot = 3 * way + kind
        return remote(
            view, view, ag_send.at[n, slot], ag_recv.at[n, slot],
            dev(illum=il_next if way == 0 else il_prev),
        )

    pending = []

    def go(copy):
        copy.start()
        pending.append(copy)

    def start_chunk(copy):
        copy.start()

    def edge_copy(side):
        return remote(
            edge_src.at[side], ext.at[i, pl.ds(16 * (1 - side), 16), :], edge_send.at[side], edge_recv.at[side],
            dev(gy=add(j, 2 * side - 1, n_gy)),
        )

    def lab_col_copy(side, slot):
        return remote(
            pack_lab.at[side], ext.at[i, pl.ds(32, 16), pl.ds(128 * slot, 128)],
            cl_send.at[slot], cl_recv.at[slot], dev(gy=add(j, 1 - slot, n_gy), gx=add(g, 2 * side - 1, n_gx)),
        )

    def ext_copy(d):
        view = ext.at[i, pl.ds(0, 32), :]
        return remote(view, view, ext_send.at[d - 1], ext_recv.at[d - 1], dev(illum=add(i, d, n_il)))

    def ext_col_copy(d, source):
        view = ext.at[source, pl.ds(32, 16), pl.ds(0, 384)]
        return remote(
            view, view, extc_send.at[d - 1], extc_recv.at[lax.rem(source, 2)], dev(illum=add(i, d, n_il))
        )

    def row_copy(side):
        src = inc.at[:, pl.ds(0 if side == 0 else cy - 8, 8), :]
        return remote(
            src, rowbuf.at[1 - side], row_send.at[side], row_recv.at[side], dev(gy=add(j, 2 * side - 1, n_gy))
        )

    def col_copy(side, slot):
        return remote(
            pack_fld.at[side], colbuf.at[1 - side, slot], col_send.at[side, slot], col_recv.at[side, slot],
            dev(gy=add(j, 1 - slot, n_gy), gx=add(g, 2 * side - 1, n_gx)),
        )

    def send_own(n):
        for kind in range(2):
            for way in range(2):
                start_chunk(chunk_copy(n, way, kind, i))

    def forward(n):
        for way in range(2):
            src = il_prev if way == 0 else il_next
            chunk_copy(n, way, 0, src).wait_recv()
            start_chunk(chunk_copy(n, way, 2, src))

    def arrived(n):
        for way in range(2):
            chunk_copy(n, way, 2, il_far).wait_recv()

    def near(n):
        for way in range(2):
            chunk_copy(n, way, 1, il_prev if way == 0 else il_next).wait_recv()

    up_ok, down_ok = j > 0, j < n_gy - 1
    left_ok, right_ok = g > 0, g < n_gx - 1

    def assemble_field(h):
        first = h * size
        for f in range(2):
            def main(c, carry):
                lanes = pl.ds(pl.multiple_of(c * 128, 128), 128)
                fld[f][c, 0:8, :] = jnp.zeros((8, 128), F32)
                fld[f][c, size + 24 : size + 32, :] = jnp.zeros((8, 128), F32)
                fld[f][c, 16 : size + 16, :] = stage[f, first : first + size, lanes]
                if h == 0:
                    fld[f][c, 8:16, :] = only_if(up_ok, rowbuf[0, f, :, lanes], 0.0)
                else:
                    fld[f][c, 8:16, :] = stage[f, first - 8 : first, lanes]
                if h == parts - 1:
                    fld[f][c, size + 16 : size + 24, :] = only_if(down_ok, rowbuf[1, f, :, lanes], 0.0)
                else:
                    fld[f][c, size + 16 : size + 24, :] = stage[f, first + size : first + size + 8, lanes]
                return carry

            lax.fori_loop(0, tiles, main, 0)
            fld[f][tiles, 0:8, :] = jnp.zeros((8, 128), F32)
            fld[f][tiles, size + 24 : size + 32, :] = jnp.zeros((8, 128), F32)

        def put(f, row, value):
            fld[f][tiles, row : row + 8, :] = value

        for f in range(2):
            edge_tiles(
                h, 0.0, lambda side, slot: colbuf[side, slot, f], lambda row, value: put(f, row, value)
            )

    def edge_tiles(h, fill, get, put):
        total = cy // 8
        for t in range(h * size // 8 - 1, (h + 1) * size // 8 + 1):
            slot, rank, ok = (0, total - 1, up_ok) if t < 0 else (2, 0, down_ok) if t >= total else (1, t, None)
            both = (left_ok, right_ok) if ok is None else (left_ok & ok, right_ok & ok)
            value = unpack_edges(get(0, slot), get(1, slot), rank, fill, *both)
            put(16 + 8 * t - h * size, value)

    def set_coefs(s, c, row, rows, label):
        a, b = coefficients(label)
        swing[s, c, row : row + rows, :] = a
        damp[s, c, row : row + rows, :] = b

    def quarter_coefs(s, q):
        def main(tile, carry):
            lanes = pl.ds(pl.multiple_of(tile * 128, 128), 128)
            set_coefs(s, q * per_q + tile, 16, cy, labs[q, s, :, lanes].astype(F32))
            return carry

        lax.fori_loop(0, per_q, main, 0)

    def halo_coefs(s):
        def main(c, carry):
            q = c // per_q
            lanes = pl.ds(pl.multiple_of(lax.rem(c, per_q) * 128, 128), 128)
            for row, first, ok in ((8, 0, up_ok), (cy + 16, 16, down_ok)):
                label = ext[q, first : first + 16, lanes].astype(F32)[8 * s : 8 * s + 8]
                set_coefs(s, c, row, 8, only_if(ok, label, -1.0))
            return carry

        lax.fori_loop(0, tiles, main, 0)

        def get(side, slot):
            both = ext[n_il - 1 if side == 0 else 0, 32:48, 128 * slot : 128 * slot + 128].astype(F32)
            return both[8 * s : 8 * s + 8]

        edge_tiles(0, -1.0, get, lambda row, value: set_coefs(s, tiles, row, 8, value))

    def half_step(s, target, source, sign):
        rows = (size + 16) // 2
        lane = lane_ids(rows)
        for part in range(2):
            r = 8 + rows * part
            before, mid = source[tiles, r : r + rows, :], source[0, r : r + rows, :]
            for c in range(tiles + 1):
                after = source[(c + 1) % (tiles + 1), r : r + rows, :]
                vert = source[c, r - 1 : r - 1 + rows, :] + source[c, r + 1 : r + 1 + rows, :]
                left = pltpu.roll(jnp.where(lane == 127, before, mid), 1, 1)
                right = pltpu.roll(jnp.where(lane == 0, after, mid), 127, 1)
                total = vert + (left + right) + swing[s, c, r : r + rows, :] * mid
                target[c, r : r + rows, :] = damp[s, c, r : r + rows, :] * (target[c, r : r + rows, :] + (sign * RATE) * total)
                before, mid = mid, after

    def transform(h):
        first = h * size

        def modulate(c, carry):
            lanes = pl.ds(pl.multiple_of(c * 128, 128), 128)
            cos = jnp.concatenate([turn[0, c]] * (size // 8))
            sin = jnp.concatenate([turn[1, c]] * (size // 8))
            real = fld[0][c, 16 : size + 16, :]
            imag = fld[1][c, 16 : size + 16, :]
            out_stage[0, first : first + size, lanes] = real
            out_stage[1, first : first + size, lanes] = imag
            for n, value in enumerate((real * cos - imag * sin, real * sin + imag * cos)):
                high = value.astype(BF16)
                lhs[0, n * size : (n + 1) * size, lanes] = high
                lhs[1, n * size : (n + 1) * size, lanes] = (value - high.astype(F32)).astype(BF16)
            return carry

        lax.fori_loop(0, tiles, modulate, 0)
        pltpu.make_async_copy(
            out_stage.at[:, pl.ds(first, size), :], exit_ref.at[:, pl.ds(first, size), :], sem_out.at[h]
        ).start()
        lane = lane_ids(8)
        first_m = jnp.where((g == 0) | (g == n_gx - 1), 0, 1)
        for turn_no in range(det // 256):
            m = first_m + turn_no - 2 * first_m * turn_no
            cols = pl.ds(pl.multiple_of(256 * m, 256), 256)
            prod = jnp.dot(lhs[0], wx[0, :, cols], preferred_element_type=F32)
            prod += jnp.dot(lhs[1], wx[0, :, cols], preferred_element_type=F32)
            prod += jnp.dot(lhs[0], wx[1, :, cols], preferred_element_type=F32)
            c_re, s_re = prod[:size, :128], prod[:size, 128:]
            c_im, s_im = prod[size:, :128], prod[size:, 128:]
            rank = 128 * m + lane
            for block, freq, g_re, g_im in (
                (n_gx // 2 + m, rank, c_re + s_im, c_im - s_re),
                (n_gx // 2 - 1 - m, -rank - 1, c_re - s_im, c_im + s_re),
            ):
                quarter = lax.rem((freq + det) * g, n_gx) * (4 // n_gx)
                f_re = jnp.where(quarter == 0, 1.0, jnp.where(quarter == 2, -1.0, 0.0))
                f_im = jnp.where(quarter == 1, -1.0, jnp.where(quarter == 3, 1.0, 0.0))
                f_re = jnp.concatenate([f_re] * (size // 8))
                f_im = jnp.concatenate([f_im] * (size // 8))
                real, imag = g_re * f_re - g_im * f_im, g_re * f_im + g_im * f_re
                gown[block, 0:size, :] = real
                gown[block, size : 2 * size, :] = imag
                head, real, imag = encode(real, imag)
                gsend[block, h, 0:16, :] = head
                gsend[block, h, 16 : 16 + size, :] = real
                gsend[block, h, 16 + size : 16 + 2 * size, :] = imag
            opposite = add(g, 2, n_gx)
            if turn_no == 0:
                g_copy(h, 2).start()
                other = 2 * (n_gx // 2) - 1 - opposite
            else:
                other = 2 * (n_gx // 2) - 1 - g
            @pl.when(other != g)
            def _():
                g_copy(h, lax.rem(other - g + n_gx, n_gx)).start()

    def g_copy(h, d):
        block = add(g, d, n_gx)
        return remote(
            gsend.at[block, h], grecv.at[d - 1, h], g_send.at[h, d - 1], g_recv.at[h, d - 1], dev(gx=block)
        )

    def g_total(h):
        real, imag = gown[g, 0:size, :], gown[g, size : 2 * size, :]
        for d in range(1, n_gx):
            g_copy(h, d).wait_recv()
            more = decode(grecv[d - 1, h], size)
            real, imag = real + more[0], imag + more[1]
        return real, imag

    own_labels(0)
    pl.semaphore_wait(barrier, len(peers))
    send_own(0)
    own_labels(1)
    label_edges()
    for side, owner in ((0, 0), (1, n_il - 1)):
        @pl.when(i == owner)
        def _():
            for slot in range(3):
                lab_col_copy(side, slot).start()
    for side in range(2):
        go(edge_copy(side))
    for side in range(2):
        go(row_copy(side))
    load_fld.wait()
    for f in range(2):
        pack_fld[0, f] = pack_edge(stage[f, :, 0:128], False)
        pack_fld[1, f] = pack_edge(stage[f, :, cx - 128 : cx], True)
    for side in range(2):
        for slot in range(3):
            go(col_copy(side, slot))
    forward(0)
    for side in range(2):
        edge_copy(side).wait_recv()
    @pl.when((i == 0) | (i == n_il - 1))
    def _():
        for slot in range(3):
            lab_col_copy(0, slot).wait_recv()
        for d in range(1, n_il):
            ext_col_copy(d, i).start()
    for d in range(1, n_il):
        go(ext_copy(d))
    send_own(1)
    quarter_coefs(0, i)
    quarter_coefs(1, i)
    near(0)
    quarter_coefs(0, il_prev)
    quarter_coefs(0, il_next)
    for side in range(2):
        row_copy(side).wait_recv()
        for slot in range(3):
            col_copy(side, slot).wait_recv()
    assemble_field(0)
    for d in range(1, n_il):
        ext_copy(d).wait_recv()
    for owner in (0, n_il - 1):
        @pl.when(i != owner)
        def _():
            ext_col_copy(1, owner).wait_recv()
    for s in range(slices):
        halo_coefs(s)
    arrived(0)
    quarter_coefs(0, il_far)
    for s in range(slices):
        def substep(step, carry):
            if s == 0:
                @pl.when(step == 1)
                def _():
                    forward(1)

            half_step(s, fld[0], fld[1], -1.0)
            half_step(s, fld[1], fld[0], 1.0)
            return carry

        lax.fori_loop(0, SUB, substep, 0)
        if s == 0:
            near(1)
            quarter_coefs(1, il_prev)
            quarter_coefs(1, il_next)
            arrived(1)
            quarter_coefs(1, il_far)
    load_turn.wait()
    load_wx.wait()
    transform(0)

    load_ey.wait()
    for h in range(parts):
        for col, value in enumerate(g_total(h)):
            high = value.astype(BF16)
            low = (value - high.astype(F32)).astype(BF16)
            for n, piece in enumerate((high, low)):
                rhs[n, 0:cy, 128 * col : 128 * col + 128] = piece
                if col == 0:
                    rhs[n, cy : 2 * cy, 128:256] = -piece
                else:
                    rhs[n, cy : 2 * cy, 0:128] = piece

    share = det // n_gy
    half = det // 2
    odd = lax.rem(j, 2)

    def wave_rows(parity):
        rows = pl.ds(pl.multiple_of(parity * half, half), half)
        return (
            jnp.dot(ey[0, rows, :], rhs[0], preferred_element_type=F32)
            + jnp.dot(ey[1, rows, :], rhs[0], preferred_element_type=F32)
            + jnp.dot(ey[0, rows, :], rhs[1], preferred_element_type=F32)
        )

    def pair_copy(k):
        rows = pl.ds(k * half // 2, half // 2)
        return remote(
            fsend.at[rows, :], fpair.at[rows, :], pair_send.at[k], pair_recv.at[k], dev(gy=j + 1 - 2 * odd)
        )

    fsend[...] = wave_rows(1 - odd)
    for k in range(2):
        go(pair_copy(k))
    fhalf[...] = wave_rows(odd)
    for k in range(2):
        pair_copy(k).wait_recv()
    fhalf[...] += fpair[...]
    head, real, imag = encode(fhalf[:, 0:128], fhalf[:, 128:256])
    for k in range(n_gy // 2):
        rows = slice(k * share, (k + 1) * share)
        fcode[k, 0:16, :] = head
        fcode[k, 16 : 16 + share, :] = real[rows]
        fcode[k, 16 + share : 16 + 2 * share, :] = imag[rows]

    def f_copy(d):
        there = add(j, d, n_gy)
        return remote(
            fcode.at[there // 2], frecv.at[d // 2 - 1], f_send.at[d // 2 - 1], f_recv.at[d // 2 - 1], dev(gy=there)
        )

    order = sorted(range(2, n_gy, 2), key=lambda d: (abs(d - n_gy // 2), d))
    for d in order:
        go(f_copy(d))
    own = pl.ds(pl.multiple_of(j // 2 * share, share), share)
    acc = [fhalf[own, 0:128], fhalf[own, 128:256]]
    for d in order:
        f_copy(d).wait_recv()
        more = decode(frecv[d // 2 - 1], share)
        acc = [acc[0] + more[0], acc[1] + more[1]]
    row_id = lax.broadcasted_iota(jnp.int32, (128, 128), 0)
    col_id = lax.broadcasted_iota(jnp.int32, (128, 128), 1)
    mirror = jnp.full((128, 128), (g < n_gx // 2).astype(jnp.int32), jnp.int32)
    places = jnp.where(jnp.where(mirror > 0, 127 - col_id, col_id) == row_id, 1.0, 0.0)
    for n in range(2):
        far_ref[n] = jnp.dot(
            acc[n], places, precision=lax.Precision.HIGHEST, preferred_element_type=F32
        )

    for copy in pending:
        copy.wait_send()
    for n in range(len(chunks)):
        for way in range(2):
            for kind in range(3):
                chunk_copy(n, way, kind, i).wait_send()
    for h in range(parts):
        for d in range(1, n_gx):
            g_copy(h, d).wait_send()
    @pl.when((i == 0) | (i == n_il - 1))
    def _():
        for slot in range(3):
            lab_col_copy(0, slot).wait_send()
        for d in range(1, n_il):
            ext_col_copy(d, i).wait_send()
    for h in range(parts):
        rows = pl.ds(h * size, size)
        pltpu.make_async_copy(out_stage.at[:, rows, :], exit_ref.at[:, rows, :], sem_out.at[h]).wait()


def on_device(dims, det, incident, labels):
    n_il, n_gy, n_gx = dims
    slices, cy = labels.shape[:2]
    hbm_spec = pl.BlockSpec(memory_space=pltpu.HBM)
    qx = labels.shape[4]
    cx = incident.shape[3]
    ny, nx = cy * n_gy, cx * n_gx
    wave_x, turn, wave_y = tables(det, cy, cx, ny, nx)
    tiles = cx // 128
    size = cy // PARTS
    share = det // n_gy
    n_chunks = len(chunks_of(slices, cy, PARTS))
    dma = pltpu.SemaphoreType.DMA
    vmem = pltpu.VMEM
    any_spec = pl.BlockSpec(memory_space=pl.ANY)
    vmem_spec = pl.BlockSpec(memory_space=pltpu.VMEM)
    field, far = pl.pallas_call(
        functools.partial(kernel, dims),
        out_shape=(
            pltpu.VMEM((2, cy, cx), F32),
            pltpu.VMEM((2, share, 128), F32),
        ),
        in_specs=[hbm_spec] * 5,
        out_specs=(any_spec, vmem_spec),
        scratch_shapes=[
            vmem((slices * cy * qx // 128, 128), jnp.int32),
            vmem((2, cy, cx), F32),
            vmem((2, cy, cx), F32),
            vmem((n_il, slices, cy, qx), BF16),
            vmem((2, 8 * slices, qx), BF16),
            vmem((2, 8 * slices, 128), BF16),
            vmem((n_il, 24 * slices, qx), BF16),
            vmem((2, 2, 8, cx), F32),
            vmem((2, 2, 8, 128), F32),
            vmem((2, 3, 2, 8, 128), F32),
            vmem((tiles + 1, size + 32, 128), F32),
            vmem((tiles + 1, size + 32, 128), F32),
            vmem((slices, tiles + 1, size + 32, 128), F32),
            vmem((slices, tiles + 1, size + 32, 128), F32),
            vmem((2, tiles, 8, 128), F32),
            vmem((2, 2 * size, cx), BF16),
            vmem((2, cx, det), BF16),
            vmem((2, det, 2 * cy), BF16),
            vmem((n_gx, 2 * cy, 128), F32),
            vmem((n_gx, PARTS, 16 + 2 * size, 128), jnp.int16),
            vmem((n_gx - 1, PARTS, 16 + 2 * size, 128), jnp.int16),
            vmem((2, 2 * cy, 256), BF16),
            vmem((det // 2, 256), F32),
            vmem((det // 2, 256), F32),
            vmem((det // 2, 256), F32),
            vmem((n_gy // 2, 16 + 2 * share, 128), jnp.int16),
            vmem((n_gy // 2 - 1, 16 + 2 * share, 128), jnp.int16),
            dma((slices,)),
            dma((5,)),
            dma((PARTS,)),
            dma((n_chunks, 6)),
            dma((n_chunks, 6)),
            dma((2,)),
            dma((2,)),
            dma((3,)),
            dma((3,)),
            dma((n_il - 1,)),
            dma((n_il - 1,)),
            dma((n_il - 1,)),
            dma((2,)),
            dma((2,)),
            dma((2,)),
            dma((2, 3)),
            dma((2, 3)),
            dma((PARTS, n_gx - 1)),
            dma((PARTS, n_gx - 1)),
            dma((2,)),
            dma((2,)),
            dma((n_gy // 2 - 1,)),
            dma((n_gy // 2 - 1,)),
        ],
        compiler_params=pltpu.CompilerParams(
            collective_id=0, has_side_effects=True, vmem_limit_bytes=48 * 1024 * 1024
        ),
    )(
        *(
            pltpu.with_memory_space_constraint(x, pltpu.HBM)
            for x in (
                incident.reshape(2, cy, cx),
                labels.reshape(slices * cy * qx // 128, 128),
                jnp.asarray(wave_x),
                jnp.asarray(wave_y),
                jnp.asarray(turn),
            )
        )
    )
    return field[None], far[None]


def solution(mesh, det=DET):
    dims = tuple(mesh.shape[name] for name in ("illum", "gy", "gx"))
    in_specs = (P("illum", None, "gy", "gx"), P(None, "gy", "gx", "illum", None))
    out_specs = (P("illum", None, "gy", "gx"), P("illum", None, "gy", "gx"))
    return jax.shard_map(
        functools.partial(on_device, dims, det), mesh=mesh, in_specs=in_specs, out_specs=out_specs, check_vma=False
    )
```

```python
import functools
import math

import jax
import jax.numpy as jnp
import ml_dtypes
import numpy as np
from jax import lax
from jax.experimental import pallas as pl
from jax.experimental.pallas import tpu as pltpu
from jax.sharding import PartitionSpec as P

MESH = pl.DeviceIdType.MESH
SUB = 2
DET = 512
RATE = 0.24
PARTS = 1
F32 = jnp.float32
BF16 = jnp.bfloat16


def split(values):
    high = values.astype(ml_dtypes.bfloat16)
    low = (values - high.astype(np.float64)).astype(ml_dtypes.bfloat16)
    return np.stack([high, low])


def tables(det, cy, cx, ny, nx):
    cols = np.arange(cx)
    kappa = np.arange(det // 2) + 0.5
    angle = 2.0 * math.pi * cols[:, None] * kappa[None, :] / nx
    cos, sin = np.cos(angle), np.sin(angle)
    blocks = []
    for m in range(det // 256):
        blocks += [cos[:, 128 * m : 128 * m + 128], sin[:, 128 * m : 128 * m + 128]]
    wave_x = split(np.concatenate(blocks, axis=1))
    shift = math.pi * cols / nx
    turn = np.stack([np.cos(shift), np.sin(shift)]).astype(np.float32)
    turn = np.broadcast_to(turn.reshape(2, cx // 128, 1, 128), (2, cx // 128, 8, 128)).copy()
    share = det // (ny // cy)
    ky = (np.arange(det) - det // 2).reshape(-1, 2, share).transpose(1, 0, 2).reshape(-1)
    waves = []
    for tile in range(ny // cy):
        rows = tile * cy + np.arange(cy)
        angle = 2.0 * math.pi * ((ky[:, None] * rows[None, :]) % ny) / ny
        both = np.concatenate([np.cos(angle), np.sin(angle)], axis=1)
        waves.append(split(both / math.sqrt(ny * nx)))
    return wave_x, turn, np.stack(waves)


def lane_ids(rows):
    return lax.broadcasted_iota(jnp.int32, (rows, 128), 1)


def only_if(ok, value, other):
    flags = jnp.full(value.shape, ok.astype(jnp.int32), jnp.int32)
    return jnp.where(flags > 0, value, other)


def pack_edge(tiles, right):
    lane = lane_ids(8)
    out = jnp.zeros((8, 128), F32)
    for t in range(tiles.shape[0] // 8):
        piece = tiles[8 * t : 8 * t + 8]
        shift = (8 * t + (8 if right else 0)) % 128
        if shift:
            piece = pltpu.roll(piece, shift, 1)
        out = jnp.where(lane // 8 == t, piece, out)
    return out


def unpack_edges(left, right, t, fill, left_ok, right_ok):
    lane = lane_ids(8)
    shift_l, shift_r = (120 - 8 * t) % 128, (128 - 8 * t) % 128
    left = pltpu.roll(left, shift_l, 1) if shift_l else left
    right = pltpu.roll(right, shift_r, 1) if shift_r else right
    left = only_if(left_ok, left, fill)
    right = only_if(right_ok, right, fill)
    return jnp.where(lane < 8, right, jnp.where(lane >= 120, left, fill))


def coefficients(label):
    last = label > 6.5
    swing = jnp.where(last, 8.0, label) * (1.0 / (32.0 * RATE)) - 4.0
    loss = label + jnp.maximum(label - 4.0, 0.0) + jnp.where(last, 6.0, 0.0)
    damp = jnp.where(label < -0.5, 0.0, 1.0 - loss * (1.0 / 256.0))
    return swing, damp


def encode(real, imag):
    levels, bodies = [], []
    for value in (real, imag):
        top = jnp.maximum(jnp.max(jnp.abs(value), axis=0, keepdims=True), 2.0**-110)
        level = jnp.ceil(jnp.log2(top) * 128.0)
        levels.append(level)
        bodies.append(jnp.round(value * (jnp.exp2(level * (-1.0 / 128.0)) * 32000.0)).astype(jnp.int32).astype(jnp.int16))
    row = lax.broadcasted_iota(jnp.int32, (16, 128), 0)
    shape = (16, 128)
    head = jnp.where(row == 0, jnp.broadcast_to(levels[0], shape), jnp.broadcast_to(levels[1], shape))
    return head.astype(jnp.int32).astype(jnp.int16), bodies[0], bodies[1]


def decode(block, rows):
    unit = jnp.exp2(block[0:16].astype(jnp.int32).astype(F32) * (1.0 / 128.0)) * (1.0 / 32000.0)
    return [
        block[16 + n * rows : 16 + (n + 1) * rows].astype(jnp.int32).astype(F32) * unit[n : n + 1] for n in range(2)
    ]


def chunks_of(slices, cy, parts):
    if parts == 1:
        return [(s, 0, cy) for s in range(slices)]
    cut = cy // 2 + 16
    return [(s, a, b) for a, b in ((0, cut), (cut, cy)) for s in range(slices)]


def middle(n, a, b):
    step = (b - a) // 32 * 16
    return b - step if n % 2 else a + step


def kernel(
    dims, inc, lab, wx_hbm, ey_hbm, turn_hbm, exit_ref, far_ref,
    lab_in, stage, out_stage, labs, edge_src, pack_lab, ext, rowbuf, pack_fld, colbuf,
    fld_re, fld_im, swing, damp, turn, lhs, wx, ey, gown, gsend, grecv, rhs, fsend, fpair, fhalf, fcode, frecv,
    sem_lab, sem_in, sem_out, ag_send, ag_recv, edge_send, edge_recv, cl_send, cl_recv, ext_send, ext_recv, extc_send, extc_recv,
    row_send, row_recv, col_send, col_recv, g_send, g_recv, pair_send, pair_recv, f_send, f_recv,
):
    n_il, n_gy, n_gx = dims
    fld = (fld_re, fld_im)
    i, j, g = lax.axis_index("illum"), lax.axis_index("gy"), lax.axis_index("gx")
    _, slices, cy, qx = labs.shape
    cx = inc.shape[2]
    tiles = cx // 128
    per_q = qx // 128
    det = wx.shape[2]
    parts = PARTS
    size = cy // parts

    def dev(illum=None, gy=None, gx=None):
        return (
            i if illum is None else illum,
            j if gy is None else gy,
            g if gx is None else gx,
        )

    def add(value, step, count):
        return lax.rem(value + (step + count), count)

    def remote(src, dst, send, recv, target):
        return pltpu.make_async_remote_copy(
            src_ref=src, dst_ref=dst, send_sem=send, recv_sem=recv,
            device_id=target, device_id_type=MESH,
        )

    lab_rows = cy * per_q
    load_lab = [
        pltpu.make_async_copy(
            lab.at[pl.ds(s * lab_rows, lab_rows), :], lab_in.at[pl.ds(s * lab_rows, lab_rows), :], sem_lab.at[s]
        )
        for s in range(slices)
    ]
    load_fld = pltpu.make_async_copy(inc, stage, sem_in.at[1])
    load_wx = pltpu.make_async_copy(wx_hbm, wx, sem_in.at[2])
    load_ey = pltpu.make_async_copy(ey_hbm.at[j], ey, sem_in.at[3])
    load_turn = pltpu.make_async_copy(turn_hbm, turn, sem_in.at[4])
    for load in load_lab:
        load.start()
    load_fld.start()

    barrier = pltpu.get_barrier_semaphore()
    peers = [dev(illum=add(i, d, n_il)) for d in range(1, n_il)]
    peers += [
        dev(gy=add(j, dj, n_gy), gx=add(g, dg, n_gx))
        for dj in (-1, 0, 1) for dg in (-1, 0, 1) if dj or dg
    ]
    peers += [dev(gx=add(g, d, n_gx)) for d in range(2, n_gx - 1)]
    peers += [dev(gy=add(j, d, n_gy)) for d in range(2, n_gy, 2)]
    for peer in peers:
        pl.semaphore_signal(barrier, inc=1, device_id=peer, device_id_type=MESH)
    load_turn.start()
    load_wx.start()
    load_ey.start()

    def label_tile(s, row, rows, tile):
        return lab_in[pl.ds((s * cy + row) * per_q + tile, rows, stride=per_q), :].astype(F32)

    def own_labels(s):
        load_lab[s].wait()
        for tile in range(per_q):
            labs[i, s, :, 128 * tile : 128 * tile + 128] = label_tile(s, 0, cy, tile).astype(BF16)

    def label_edges():
        for e, top in ((0, 0), (1, cy - 8)):
            for tile in range(per_q):
                both = jnp.concatenate([label_tile(s, top, 8, tile) for s in range(slices)])
                edge_src[e, :, 128 * tile : 128 * tile + 128] = both.astype(BF16)
        for side, tile in ((0, 0), (1, per_q - 1)):
            both = jnp.concatenate([pack_edge(label_tile(s, 0, cy, tile), side == 1) for s in range(slices)])
            pack_lab[side] = both.astype(BF16)

    chunks = chunks_of(slices, cy, parts)
    il_next, il_prev = add(i, 1, n_il), add(i, -1, n_il)
    il_far = add(i, 2, n_il)

    def chunk_copy(n, way, kind, quarter):
        s, a, b = chunks[n]
        mid = middle(n, a, b)
        a, b = (a, mid) if (way == 0) == (kind != 1) else (mid, b)
        view = labs.at[quarter, s, pl.ds(a, b - a), :]
        slot = 3 * way + kind
        return remote(
            view, view, ag_send.at[n, slot], ag_recv.at[n, slot],
            dev(illum=il_next if way == 0 else il_prev),
        )

    pending = []

    def go(copy):
        copy.start()
        pending.append(copy)

    def start_chunk(copy):
        copy.start()

    def edge_copy(side):
        return remote(
            edge_src.at[side], ext.at[i, pl.ds(16 * (1 - side), 16), :], edge_send.at[side], edge_recv.at[side],
            dev(gy=add(j, 2 * side - 1, n_gy)),
        )

    def lab_col_copy(side, slot):
        return remote(
            pack_lab.at[side], ext.at[i, pl.ds(32, 16), pl.ds(128 * slot, 128)],
            cl_send.at[slot], cl_recv.at[slot], dev(gy=add(j, 1 - slot, n_gy), gx=add(g, 2 * side - 1, n_gx)),
        )

    def ext_copy(d):
        view = ext.at[i, pl.ds(0, 32), :]
        return remote(view, view, ext_send.at[d - 1], ext_recv.at[d - 1], dev(illum=add(i, d, n_il)))

    def ext_col_copy(d, source):
        view = ext.at[source, pl.ds(32, 16), pl.ds(0, 384)]
        return remote(
            view, view, extc_send.at[d - 1], extc_recv.at[lax.rem(source, 2)], dev(illum=add(i, d, n_il))
        )

    def row_copy(side):
        src = inc.at[:, pl.ds(0 if side == 0 else cy - 8, 8), :]
        return remote(
            src, rowbuf.at[1 - side], row_send.at[side], row_recv.at[side], dev(gy=add(j, 2 * side - 1, n_gy))
        )

    def col_copy(side, slot):
        return remote(
            pack_fld.at[side], colbuf.at[1 - side, slot], col_send.at[side, slot], col_recv.at[side, slot],
            dev(gy=add(j, 1 - slot, n_gy), gx=add(g, 2 * side - 1, n_gx)),
        )

    def send_own(n):
        for kind in range(2):
            for way in range(2):
                start_chunk(chunk_copy(n, way, kind, i))

    def forward(n):
        for way in range(2):
            src = il_prev if way == 0 else il_next
            chunk_copy(n, way, 0, src).wait_recv()
            start_chunk(chunk_copy(n, way, 2, src))

    def arrived(n):
        for way in range(2):
            chunk_copy(n, way, 2, il_far).wait_recv()

    def near(n):
        for way in range(2):
            chunk_copy(n, way, 1, il_prev if way == 0 else il_next).wait_recv()

    up_ok, down_ok = j > 0, j < n_gy - 1
    left_ok, right_ok = g > 0, g < n_gx - 1

    def assemble_field(h):
        first = h * size
        for f in range(2):
            def main(c, carry):
                lanes = pl.ds(pl.multiple_of(c * 128, 128), 128)
                fld[f][c, 0:8, :] = jnp.zeros((8, 128), F32)
                fld[f][c, size + 24 : size + 32, :] = jnp.zeros((8, 128), F32)
                fld[f][c, 16 : size + 16, :] = stage[f, first : first + size, lanes]
                if h == 0:
                    fld[f][c, 8:16, :] = only_if(up_ok, rowbuf[0, f, :, lanes], 0.0)
                else:
                    fld[f][c, 8:16, :] = stage[f, first - 8 : first, lanes]
                if h == parts - 1:
                    fld[f][c, size + 16 : size + 24, :] = only_if(down_ok, rowbuf[1, f, :, lanes], 0.0)
                else:
                    fld[f][c, size + 16 : size + 24, :] = stage[f, first + size : first + size + 8, lanes]
                return carry

            lax.fori_loop(0, tiles, main, 0)
            fld[f][tiles, 0:8, :] = jnp.zeros((8, 128), F32)
            fld[f][tiles, size + 24 : size + 32, :] = jnp.zeros((8, 128), F32)

        def put(f, row, value):
            fld[f][tiles, row : row + 8, :] = value

        for f in range(2):
            edge_tiles(
                h, 0.0, lambda side, slot: colbuf[side, slot, f], lambda row, value: put(f, row, value)
            )

    def edge_tiles(h, fill, get, put):
        total = cy // 8
        for t in range(h * size // 8 - 1, (h + 1) * size // 8 + 1):
            slot, rank, ok = (0, total - 1, up_ok) if t < 0 else (2, 0, down_ok) if t >= total else (1, t, None)
            both = (left_ok, right_ok) if ok is None else (left_ok & ok, right_ok & ok)
            value = unpack_edges(get(0, slot), get(1, slot), rank, fill, *both)
            put(16 + 8 * t - h * size, value)

    def set_coefs(s, c, row, rows, label):
        a, b = coefficients(label)
        swing[s, c, row : row + rows, :] = a
        damp[s, c, row : row + rows, :] = b

    def quarter_coefs(s, q):
        def main(tile, carry):
            lanes = pl.ds(pl.multiple_of(tile * 128, 128), 128)
            set_coefs(s, q * per_q + tile, 16, cy, labs[q, s, :, lanes].astype(F32))
            return carry

        lax.fori_loop(0, per_q, main, 0)

    def halo_coefs(s):
        def main(c, carry):
            q = c // per_q
            lanes = pl.ds(pl.multiple_of(lax.rem(c, per_q) * 128, 128), 128)
            for row, first, ok in ((8, 0, up_ok), (cy + 16, 16, down_ok)):
                label = ext[q, first : first + 16, lanes].astype(F32)[8 * s : 8 * s + 8]
                set_coefs(s, c, row, 8, only_if(ok, label, -1.0))
            return carry

        lax.fori_loop(0, tiles, main, 0)

        def get(side, slot):
            both = ext[n_il - 1 if side == 0 else 0, 32:48, 128 * slot : 128 * slot + 128].astype(F32)
            return both[8 * s : 8 * s + 8]

        edge_tiles(0, -1.0, get, lambda row, value: set_coefs(s, tiles, row, 8, value))

    def half_step(s, target, source, sign):
        rows = (size + 16) // 2
        lane = lane_ids(rows)
        for part in range(2):
            r = 8 + rows * part
            before, mid = source[tiles, r : r + rows, :], source[0, r : r + rows, :]
            for c in range(tiles + 1):
                after = source[(c + 1) % (tiles + 1), r : r + rows, :]
                vert = source[c, r - 1 : r - 1 + rows, :] + source[c, r + 1 : r + 1 + rows, :]
                left = pltpu.roll(jnp.where(lane == 127, before, mid), 1, 1)
                right = pltpu.roll(jnp.where(lane == 0, after, mid), 127, 1)
                total = vert + (left + right) + swing[s, c, r : r + rows, :] * mid
                target[c, r : r + rows, :] = damp[s, c, r : r + rows, :] * (target[c, r : r + rows, :] + (sign * RATE) * total)
                before, mid = mid, after

    def transform(h):
        first = h * size

        def modulate(c, carry):
            lanes = pl.ds(pl.multiple_of(c * 128, 128), 128)
            cos = jnp.concatenate([turn[0, c]] * (size // 8))
            sin = jnp.concatenate([turn[1, c]] * (size // 8))
            real = fld[0][c, 16 : size + 16, :]
            imag = fld[1][c, 16 : size + 16, :]
            out_stage[0, first : first + size, lanes] = real
            out_stage[1, first : first + size, lanes] = imag
            for n, value in enumerate((real * cos - imag * sin, real * sin + imag * cos)):
                high = value.astype(BF16)
                lhs[0, n * size : (n + 1) * size, lanes] = high
                lhs[1, n * size : (n + 1) * size, lanes] = (value - high.astype(F32)).astype(BF16)
            return carry

        lax.fori_loop(0, tiles, modulate, 0)
        pltpu.make_async_copy(
            out_stage.at[:, pl.ds(first, size), :], exit_ref.at[:, pl.ds(first, size), :], sem_out.at[h]
        ).start()
        lane = lane_ids(8)
        first_m = jnp.where((g == 0) | (g == n_gx - 1), 0, 1)
        for turn_no in range(det // 256):
            m = first_m + turn_no - 2 * first_m * turn_no
            cols = pl.ds(pl.multiple_of(256 * m, 256), 256)
            prod = jnp.dot(lhs[0], wx[0, :, cols], preferred_element_type=F32)
            prod += jnp.dot(lhs[1], wx[0, :, cols], preferred_element_type=F32)
            prod += jnp.dot(lhs[0], wx[1, :, cols], preferred_element_type=F32)
            c_re, s_re = prod[:size, :128], prod[:size, 128:]
            c_im, s_im = prod[size:, :128], prod[size:, 128:]
            rank = 128 * m + lane
            for block, freq, g_re, g_im in (
                (n_gx // 2 + m, rank, c_re + s_im, c_im - s_re),
                (n_gx // 2 - 1 - m, -rank - 1, c_re - s_im, c_im + s_re),
            ):
                quarter = lax.rem((freq + det) * g, n_gx) * (4 // n_gx)
                f_re = jnp.where(quarter == 0, 1.0, jnp.where(quarter == 2, -1.0, 0.0))
                f_im = jnp.where(quarter == 1, -1.0, jnp.where(quarter == 3, 1.0, 0.0))
                f_re = jnp.concatenate([f_re] * (size // 8))
                f_im = jnp.concatenate([f_im] * (size // 8))
                real, imag = g_re * f_re - g_im * f_im, g_re * f_im + g_im * f_re
                gown[block, 0:size, :] = real
                gown[block, size : 2 * size, :] = imag
                head, real, imag = encode(real, imag)
                gsend[block, h, 0:16, :] = head
                gsend[block, h, 16 : 16 + size, :] = real
                gsend[block, h, 16 + size : 16 + 2 * size, :] = imag
            opposite = add(g, 2, n_gx)
            if turn_no == 0:
                g_copy(h, 2).start()
                other = 2 * (n_gx // 2) - 1 - opposite
            else:
                other = 2 * (n_gx // 2) - 1 - g
            @pl.when(other != g)
            def _():
                g_copy(h, lax.rem(other - g + n_gx, n_gx)).start()

    def g_copy(h, d):
        block = add(g, d, n_gx)
        return remote(
            gsend.at[block, h], grecv.at[d - 1, h], g_send.at[h, d - 1], g_recv.at[h, d - 1], dev(gx=block)
        )

    def g_total(h):
        real, imag = gown[g, 0:size, :], gown[g, size : 2 * size, :]
        for d in range(1, n_gx):
            g_copy(h, d).wait_recv()
            more = decode(grecv[d - 1, h], size)
            real, imag = real + more[0], imag + more[1]
        return real, imag

    own_labels(0)
    pl.semaphore_wait(barrier, len(peers))
    send_own(0)
    own_labels(1)
    label_edges()
    for side, owner in ((0, 0), (1, n_il - 1)):
        @pl.when(i == owner)
        def _():
            for slot in range(3):
                lab_col_copy(side, slot).start()
    for side in range(2):
        go(edge_copy(side))
    for side in range(2):
        go(row_copy(side))
    load_fld.wait()
    for f in range(2):
        pack_fld[0, f] = pack_edge(stage[f, :, 0:128], False)
        pack_fld[1, f] = pack_edge(stage[f, :, cx - 128 : cx], True)
    for side in range(2):
        for slot in range(3):
            go(col_copy(side, slot))
    forward(0)
    for side in range(2):
        edge_copy(side).wait_recv()
    @pl.when((i == 0) | (i == n_il - 1))
    def _():
        for slot in range(3):
            lab_col_copy(0, slot).wait_recv()
        for d in range(1, n_il):
            ext_col_copy(d, i).start()
    for d in range(1, n_il):
        go(ext_copy(d))
    send_own(1)
    quarter_coefs(0, i)
    quarter_coefs(1, i)
    near(0)
    quarter_coefs(0, il_prev)
    quarter_coefs(0, il_next)
    for side in range(2):
        row_copy(side).wait_recv()
        for slot in range(3):
            col_copy(side, slot).wait_recv()
    assemble_field(0)
    arrived(0)
    quarter_coefs(0, il_far)
    for d in range(1, n_il):
        ext_copy(d).wait_recv()
    for owner in (0, n_il - 1):
        @pl.when(i != owner)
        def _():
            ext_col_copy(1, owner).wait_recv()
    halo_coefs(0)
    forward(1)
    for s in range(slices):
        def substep(step, carry):
            half_step(s, fld[0], fld[1], -1.0)
            half_step(s, fld[1], fld[0], 1.0)
            return carry

        lax.fori_loop(0, SUB, substep, 0)
        if s == 0:
            halo_coefs(1)
            near(1)
            quarter_coefs(1, il_prev)
            quarter_coefs(1, il_next)
            arrived(1)
            quarter_coefs(1, il_far)
    load_turn.wait()
    load_wx.wait()
    transform(0)

    load_ey.wait()
    for h in range(parts):
        for col, value in enumerate(g_total(h)):
            high = value.astype(BF16)
            low = (value - high.astype(F32)).astype(BF16)
            for n, piece in enumerate((high, low)):
                rhs[n, 0:cy, 128 * col : 128 * col + 128] = piece
                if col == 0:
                    rhs[n, cy : 2 * cy, 128:256] = -piece
                else:
                    rhs[n, cy : 2 * cy, 0:128] = piece

    share = det // n_gy
    half = det // 2
    odd = lax.rem(j, 2)

    def wave_rows(parity):
        rows = pl.ds(pl.multiple_of(parity * half, half), half)
        return (
            jnp.dot(ey[0, rows, :], rhs[0], preferred_element_type=F32)
            + jnp.dot(ey[1, rows, :], rhs[0], preferred_element_type=F32)
            + jnp.dot(ey[0, rows, :], rhs[1], preferred_element_type=F32)
        )

    def pair_copy(k):
        rows = pl.ds(k * half // 2, half // 2)
        return remote(
            fsend.at[rows, :], fpair.at[rows, :], pair_send.at[k], pair_recv.at[k], dev(gy=j + 1 - 2 * odd)
        )

    fsend[...] = wave_rows(1 - odd)
    for k in range(2):
        go(pair_copy(k))
    fhalf[...] = wave_rows(odd)
    for k in range(2):
        pair_copy(k).wait_recv()
    fhalf[...] += fpair[...]
    head, real, imag = encode(fhalf[:, 0:128], fhalf[:, 128:256])
    for k in range(n_gy // 2):
        rows = slice(k * share, (k + 1) * share)
        fcode[k, 0:16, :] = head
        fcode[k, 16 : 16 + share, :] = real[rows]
        fcode[k, 16 + share : 16 + 2 * share, :] = imag[rows]

    def f_copy(d):
        there = add(j, d, n_gy)
        return remote(
            fcode.at[there // 2], frecv.at[d // 2 - 1], f_send.at[d // 2 - 1], f_recv.at[d // 2 - 1], dev(gy=there)
        )

    order = sorted(range(2, n_gy, 2), key=lambda d: (abs(d - n_gy // 2), d))
    for d in order:
        go(f_copy(d))
    own = pl.ds(pl.multiple_of(j // 2 * share, share), share)
    acc = [fhalf[own, 0:128], fhalf[own, 128:256]]
    for d in order:
        f_copy(d).wait_recv()
        more = decode(frecv[d // 2 - 1], share)
        acc = [acc[0] + more[0], acc[1] + more[1]]
    row_id = lax.broadcasted_iota(jnp.int32, (128, 128), 0)
    col_id = lax.broadcasted_iota(jnp.int32, (128, 128), 1)
    mirror = jnp.full((128, 128), (g < n_gx // 2).astype(jnp.int32), jnp.int32)
    places = jnp.where(jnp.where(mirror > 0, 127 - col_id, col_id) == row_id, 1.0, 0.0)
    for n in range(2):
        far_ref[n] = jnp.dot(
            acc[n], places, precision=lax.Precision.HIGHEST, preferred_element_type=F32
        )

    for copy in pending:
        copy.wait_send()
    for n in range(len(chunks)):
        for way in range(2):
            for kind in range(3):
                chunk_copy(n, way, kind, i).wait_send()
    for h in range(parts):
        for d in range(1, n_gx):
            g_copy(h, d).wait_send()
    @pl.when((i == 0) | (i == n_il - 1))
    def _():
        for slot in range(3):
            lab_col_copy(0, slot).wait_send()
        for d in range(1, n_il):
            ext_col_copy(d, i).wait_send()
    for h in range(parts):
        rows = pl.ds(h * size, size)
        pltpu.make_async_copy(out_stage.at[:, rows, :], exit_ref.at[:, rows, :], sem_out.at[h]).wait()


def on_device(dims, det, incident, labels):
    n_il, n_gy, n_gx = dims
    slices, cy = labels.shape[:2]
    hbm_spec = pl.BlockSpec(memory_space=pltpu.HBM)
    qx = labels.shape[4]
    cx = incident.shape[3]
    ny, nx = cy * n_gy, cx * n_gx
    wave_x, turn, wave_y = tables(det, cy, cx, ny, nx)
    tiles = cx // 128
    size = cy // PARTS
    share = det // n_gy
    n_chunks = len(chunks_of(slices, cy, PARTS))
    dma = pltpu.SemaphoreType.DMA
    vmem = pltpu.VMEM
    any_spec = pl.BlockSpec(memory_space=pl.ANY)
    vmem_spec = pl.BlockSpec(memory_space=pltpu.VMEM)
    field, far = pl.pallas_call(
        functools.partial(kernel, dims),
        out_shape=(
            pltpu.VMEM((2, cy, cx), F32),
            pltpu.VMEM((2, share, 128), F32),
        ),
        in_specs=[hbm_spec] * 5,
        out_specs=(any_spec, vmem_spec),
        scratch_shapes=[
            vmem((slices * cy * qx // 128, 128), jnp.int32),
            vmem((2, cy, cx), F32),
            vmem((2, cy, cx), F32),
            vmem((n_il, slices, cy, qx), BF16),
            vmem((2, 8 * slices, qx), BF16),
            vmem((2, 8 * slices, 128), BF16),
            vmem((n_il, 24 * slices, qx), BF16),
            vmem((2, 2, 8, cx), F32),
            vmem((2, 2, 8, 128), F32),
            vmem((2, 3, 2, 8, 128), F32),
            vmem((tiles + 1, size + 32, 128), F32),
            vmem((tiles + 1, size + 32, 128), F32),
            vmem((slices, tiles + 1, size + 32, 128), F32),
            vmem((slices, tiles + 1, size + 32, 128), F32),
            vmem((2, tiles, 8, 128), F32),
            vmem((2, 2 * size, cx), BF16),
            vmem((2, cx, det), BF16),
            vmem((2, det, 2 * cy), BF16),
            vmem((n_gx, 2 * cy, 128), F32),
            vmem((n_gx, PARTS, 16 + 2 * size, 128), jnp.int16),
            vmem((n_gx - 1, PARTS, 16 + 2 * size, 128), jnp.int16),
            vmem((2, 2 * cy, 256), BF16),
            vmem((det // 2, 256), F32),
            vmem((det // 2, 256), F32),
            vmem((det // 2, 256), F32),
            vmem((n_gy // 2, 16 + 2 * share, 128), jnp.int16),
            vmem((n_gy // 2 - 1, 16 + 2 * share, 128), jnp.int16),
            dma((slices,)),
            dma((5,)),
            dma((PARTS,)),
            dma((n_chunks, 6)),
            dma((n_chunks, 6)),
            dma((2,)),
            dma((2,)),
            dma((3,)),
            dma((3,)),
            dma((n_il - 1,)),
            dma((n_il - 1,)),
            dma((n_il - 1,)),
            dma((2,)),
            dma((2,)),
            dma((2,)),
            dma((2, 3)),
            dma((2, 3)),
            dma((PARTS, n_gx - 1)),
            dma((PARTS, n_gx - 1)),
            dma((2,)),
            dma((2,)),
            dma((n_gy // 2 - 1,)),
            dma((n_gy // 2 - 1,)),
        ],
        compiler_params=pltpu.CompilerParams(
            collective_id=0, has_side_effects=True, vmem_limit_bytes=48 * 1024 * 1024
        ),
    )(
        *(
            pltpu.with_memory_space_constraint(x, pltpu.HBM)
            for x in (
                incident.reshape(2, cy, cx),
                labels.reshape(slices * cy * qx // 128, 128),
                jnp.asarray(wave_x),
                jnp.asarray(wave_y),
                jnp.asarray(turn),
            )
        )
    )
    return field[None], far[None]


def solution(mesh, det=DET):
    dims = tuple(mesh.shape[name] for name in ("illum", "gy", "gx"))
    in_specs = (P("illum", None, "gy", "gx"), P(None, "gy", "gx", "illum", None))
    out_specs = (P("illum", None, "gy", "gx"), P("illum", None, "gy", "gx"))
    return jax.shard_map(
        functools.partial(on_device, dims, det), mesh=mesh, in_specs=in_specs, out_specs=out_specs, check_vma=False
    )
```

```python
import functools
import math

import jax
import jax.numpy as jnp
import ml_dtypes
import numpy as np
from jax import lax
from jax.experimental import pallas as pl
from jax.experimental.pallas import tpu as pltpu
from jax.sharding import PartitionSpec as P

MESH = pl.DeviceIdType.MESH
SUB = 2
DET = 512
RATE = 0.24
PARTS = 1
F32 = jnp.float32
BF16 = jnp.bfloat16


def split(values):
    high = values.astype(ml_dtypes.bfloat16)
    low = (values - high.astype(np.float64)).astype(ml_dtypes.bfloat16)
    return np.stack([high, low])


def tables(det, cy, cx, ny, nx):
    cols = np.arange(cx)
    kappa = np.arange(det // 2) + 0.5
    angle = 2.0 * math.pi * cols[:, None] * kappa[None, :] / nx
    cos, sin = np.cos(angle), np.sin(angle)
    blocks = []
    for m in range(det // 256):
        blocks += [cos[:, 128 * m : 128 * m + 128], sin[:, 128 * m : 128 * m + 128]]
    wave_x = split(np.concatenate(blocks, axis=1))
    shift = math.pi * cols / nx
    turn = np.stack([np.cos(shift), np.sin(shift)]).astype(np.float32)
    turn = np.broadcast_to(turn.reshape(2, cx // 128, 1, 128), (2, cx // 128, 8, 128)).copy()
    share = det // (ny // cy)
    ky = (np.arange(det) - det // 2).reshape(-1, 2, share).transpose(1, 0, 2).reshape(-1)
    waves = []
    for tile in range(ny // cy):
        rows = tile * cy + np.arange(cy)
        angle = 2.0 * math.pi * ((ky[:, None] * rows[None, :]) % ny) / ny
        both = np.concatenate([np.cos(angle), np.sin(angle)], axis=1)
        waves.append(split(both / math.sqrt(ny * nx)))
    return wave_x, turn, np.stack(waves)


def lane_ids(rows):
    return lax.broadcasted_iota(jnp.int32, (rows, 128), 1)


def only_if(ok, value, other):
    flags = jnp.full(value.shape, ok.astype(jnp.int32), jnp.int32)
    return jnp.where(flags > 0, value, other)


def pack_edge(tiles, right):
    lane = lane_ids(8)
    out = jnp.zeros((8, 128), F32)
    for t in range(tiles.shape[0] // 8):
        piece = tiles[8 * t : 8 * t + 8]
        shift = (8 * t + (8 if right else 0)) % 128
        if shift:
            piece = pltpu.roll(piece, shift, 1)
        out = jnp.where(lane // 8 == t, piece, out)
    return out


def unpack_edges(left, right, t, fill, left_ok, right_ok):
    lane = lane_ids(8)
    shift_l, shift_r = (120 - 8 * t) % 128, (128 - 8 * t) % 128
    left = pltpu.roll(left, shift_l, 1) if shift_l else left
    right = pltpu.roll(right, shift_r, 1) if shift_r else right
    left = only_if(left_ok, left, fill)
    right = only_if(right_ok, right, fill)
    return jnp.where(lane < 8, right, jnp.where(lane >= 120, left, fill))


def coefficients(label):
    last = label > 6.5
    swing = jnp.where(last, 8.0, label) * (1.0 / (32.0 * RATE)) - 4.0
    loss = label + jnp.maximum(label - 4.0, 0.0) + jnp.where(last, 6.0, 0.0)
    damp = jnp.where(label < -0.5, 0.0, 1.0 - loss * (1.0 / 256.0))
    return swing, damp


def encode(real, imag):
    levels, bodies = [], []
    for value in (real, imag):
        top = jnp.maximum(jnp.max(jnp.abs(value), axis=0, keepdims=True), 2.0**-110)
        level = jnp.ceil(jnp.log2(top) * 128.0)
        levels.append(level)
        bodies.append(jnp.round(value * (jnp.exp2(level * (-1.0 / 128.0)) * 32000.0)).astype(jnp.int32).astype(jnp.int16))
    row = lax.broadcasted_iota(jnp.int32, (16, 128), 0)
    shape = (16, 128)
    head = jnp.where(row == 0, jnp.broadcast_to(levels[0], shape), jnp.broadcast_to(levels[1], shape))
    return head.astype(jnp.int32).astype(jnp.int16), bodies[0], bodies[1]


def decode(block, rows):
    unit = jnp.exp2(block[0:16].astype(jnp.int32).astype(F32) * (1.0 / 128.0)) * (1.0 / 32000.0)
    return [
        block[16 + n * rows : 16 + (n + 1) * rows].astype(jnp.int32).astype(F32) * unit[n : n + 1] for n in range(2)
    ]


def chunks_of(slices, cy, parts):
    if parts == 1:
        return [(s, 0, cy) for s in range(slices)]
    cut = cy // 2 + 16
    return [(s, a, b) for a, b in ((0, cut), (cut, cy)) for s in range(slices)]


def middle(n, a, b):
    step = (b - a) // 32 * 16
    return b - step if n % 2 else a + step


def kernel(
    dims, inc, lab, wx_hbm, ey_hbm, turn_hbm, exit_ref, far_ref,
    lab_in, stage, out_stage, labs, edge_src, pack_lab, ext, rowbuf, pack_fld, colbuf,
    fld_re, fld_im, swing, damp, turn, lhs, wx, ey, gown, gsend, grecv, rhs, fsend, fpair, fhalf, fcode, frecv,
    sem_lab, sem_in, sem_out, ag_send, ag_recv, edge_send, edge_recv, cl_send, cl_recv, ext_send, ext_recv, extc_send, extc_recv,
    row_send, row_recv, col_send, col_recv, g_send, g_recv, pair_send, pair_recv, f_send, f_recv,
):
    n_il, n_gy, n_gx = dims
    fld = (fld_re, fld_im)
    i, j, g = lax.axis_index("illum"), lax.axis_index("gy"), lax.axis_index("gx")
    _, slices, cy, qx = labs.shape
    cx = inc.shape[2]
    tiles = cx // 128
    per_q = qx // 128
    det = wx.shape[2]
    parts = PARTS
    size = cy // parts

    def dev(illum=None, gy=None, gx=None):
        return (
            i if illum is None else illum,
            j if gy is None else gy,
            g if gx is None else gx,
        )

    def add(value, step, count):
        return lax.rem(value + (step + count), count)

    def remote(src, dst, send, recv, target):
        return pltpu.make_async_remote_copy(
            src_ref=src, dst_ref=dst, send_sem=send, recv_sem=recv,
            device_id=target, device_id_type=MESH,
        )

    lab_rows = cy * per_q
    load_lab = [
        pltpu.make_async_copy(
            lab.at[pl.ds(s * lab_rows, lab_rows), :], lab_in.at[pl.ds(s * lab_rows, lab_rows), :], sem_lab.at[s]
        )
        for s in range(slices)
    ]
    load_fld = pltpu.make_async_copy(inc, stage, sem_in.at[1])
    load_wx = pltpu.make_async_copy(wx_hbm, wx, sem_in.at[2])
    load_ey = pltpu.make_async_copy(ey_hbm.at[j], ey, sem_in.at[3])
    load_turn = pltpu.make_async_copy(turn_hbm, turn, sem_in.at[4])
    for load in load_lab:
        load.start()
    load_fld.start()

    barrier = pltpu.get_barrier_semaphore()
    peers = [dev(illum=add(i, d, n_il)) for d in range(1, n_il)]
    peers += [
        dev(gy=add(j, dj, n_gy), gx=add(g, dg, n_gx))
        for dj in (-1, 0, 1) for dg in (-1, 0, 1) if dj or dg
    ]
    peers += [dev(gx=add(g, d, n_gx)) for d in range(2, n_gx - 1)]
    peers += [dev(gy=add(j, d, n_gy)) for d in range(2, n_gy, 2)]
    for peer in peers:
        pl.semaphore_signal(barrier, inc=1, device_id=peer, device_id_type=MESH)
    load_turn.start()
    load_wx.start()
    load_ey.start()

    def label_tile(s, row, rows, tile):
        return lab_in[pl.ds((s * cy + row) * per_q + tile, rows, stride=per_q), :].astype(F32)

    def own_labels(s):
        load_lab[s].wait()
        for tile in range(per_q):
            labs[i, s, :, 128 * tile : 128 * tile + 128] = label_tile(s, 0, cy, tile).astype(BF16)

    def label_edges():
        for e, top in ((0, 0), (1, cy - 8)):
            for tile in range(per_q):
                both = jnp.concatenate([label_tile(s, top, 8, tile) for s in range(slices)])
                edge_src[e, :, 128 * tile : 128 * tile + 128] = both.astype(BF16)
        for side, tile in ((0, 0), (1, per_q - 1)):
            both = jnp.concatenate([pack_edge(label_tile(s, 0, cy, tile), side == 1) for s in range(slices)])
            pack_lab[side] = both.astype(BF16)

    chunks = chunks_of(slices, cy, parts)
    il_next, il_prev = add(i, 1, n_il), add(i, -1, n_il)
    il_far = add(i, 2, n_il)

    def chunk_copy(n, way, kind, quarter):
        s, a, b = chunks[n]
        mid = middle(n, a, b)
        a, b = (a, mid) if (way == 0) == (kind != 1) else (mid, b)
        view = labs.at[quarter, s, pl.ds(a, b - a), :]
        slot = 3 * way + kind
        return remote(
            view, view, ag_send.at[n, slot], ag_recv.at[n, slot],
            dev(illum=il_next if way == 0 else il_prev),
        )

    pending = []

    def go(copy):
        copy.start()
        pending.append(copy)

    def start_chunk(copy):
        copy.start()

    def edge_copy(side):
        return remote(
            edge_src.at[side], ext.at[i, pl.ds(16 * (1 - side), 16), :], edge_send.at[side], edge_recv.at[side],
            dev(gy=add(j, 2 * side - 1, n_gy)),
        )

    def lab_col_copy(side, slot):
        return remote(
            pack_lab.at[side], ext.at[i, pl.ds(32, 16), pl.ds(128 * slot, 128)],
            cl_send.at[slot], cl_recv.at[slot], dev(gy=add(j, 1 - slot, n_gy), gx=add(g, 2 * side - 1, n_gx)),
        )

    def ext_copy(d):
        view = ext.at[i, pl.ds(0, 32), :]
        return remote(view, view, ext_send.at[d - 1], ext_recv.at[d - 1], dev(illum=add(i, d, n_il)))

    def ext_col_copy(d, source):
        view = ext.at[source, pl.ds(32, 16), pl.ds(0, 384)]
        return remote(
            view, view, extc_send.at[d - 1], extc_recv.at[lax.rem(source, 2)], dev(illum=add(i, d, n_il))
        )

    def row_copy(side):
        src = inc.at[:, pl.ds(0 if side == 0 else cy - 8, 8), :]
        return remote(
            src, rowbuf.at[1 - side], row_send.at[side], row_recv.at[side], dev(gy=add(j, 2 * side - 1, n_gy))
        )

    def col_copy(side, slot):
        return remote(
            pack_fld.at[side], colbuf.at[1 - side, slot], col_send.at[side, slot], col_recv.at[side, slot],
            dev(gy=add(j, 1 - slot, n_gy), gx=add(g, 2 * side - 1, n_gx)),
        )

    def send_own(n):
        for kind in range(2):
            for way in range(2):
                start_chunk(chunk_copy(n, way, kind, i))

    def forward(n):
        for way in range(2):
            src = il_prev if way == 0 else il_next
            chunk_copy(n, way, 0, src).wait_recv()
            start_chunk(chunk_copy(n, way, 2, src))

    def arrived(n):
        for way in range(2):
            chunk_copy(n, way, 2, il_far).wait_recv()

    def near(n):
        for way in range(2):
            chunk_copy(n, way, 1, il_prev if way == 0 else il_next).wait_recv()

    up_ok, down_ok = j > 0, j < n_gy - 1
    left_ok, right_ok = g > 0, g < n_gx - 1

    def assemble_field(h):
        first = h * size
        for f in range(2):
            rate = RATE if f else 1.0

            def main(c, carry):
                lanes = pl.ds(pl.multiple_of(c * 128, 128), 128)
                fld[f][c, 0:8, :] = jnp.zeros((8, 128), F32)
                fld[f][c, size + 24 : size + 32, :] = jnp.zeros((8, 128), F32)
                fld[f][c, 16 : size + 16, :] = stage[f, first : first + size, lanes] * rate
                if h == 0:
                    fld[f][c, 8:16, :] = only_if(up_ok, rowbuf[0, f, :, lanes], 0.0) * rate
                else:
                    fld[f][c, 8:16, :] = stage[f, first - 8 : first, lanes]
                if h == parts - 1:
                    fld[f][c, size + 16 : size + 24, :] = only_if(down_ok, rowbuf[1, f, :, lanes], 0.0) * rate
                else:
                    fld[f][c, size + 16 : size + 24, :] = stage[f, first + size : first + size + 8, lanes]
                return carry

            lax.fori_loop(0, tiles, main, 0)
            fld[f][tiles, 0:8, :] = jnp.zeros((8, 128), F32)
            fld[f][tiles, size + 24 : size + 32, :] = jnp.zeros((8, 128), F32)

        def put(f, row, value):
            fld[f][tiles, row : row + 8, :] = value

        for f in range(2):
            edge_tiles(
                h, 0.0, lambda side, slot: colbuf[side, slot, f], lambda row, value: put(f, row, value * (RATE if f else 1.0))
            )

    def edge_tiles(h, fill, get, put):
        total = cy // 8
        for t in range(h * size // 8 - 1, (h + 1) * size // 8 + 1):
            slot, rank, ok = (0, total - 1, up_ok) if t < 0 else (2, 0, down_ok) if t >= total else (1, t, None)
            both = (left_ok, right_ok) if ok is None else (left_ok & ok, right_ok & ok)
            value = unpack_edges(get(0, slot), get(1, slot), rank, fill, *both)
            put(16 + 8 * t - h * size, value)

    def set_coefs(s, c, row, rows, label):
        a, b = coefficients(label)
        swing[s, c, row : row + rows, :] = a
        damp[s, c, row : row + rows, :] = b

    def quarter_coefs(s, q):
        def main(tile, carry):
            lanes = pl.ds(pl.multiple_of(tile * 128, 128), 128)
            set_coefs(s, q * per_q + tile, 16, cy, labs[q, s, :, lanes].astype(F32))
            return carry

        lax.fori_loop(0, per_q, main, 0)

    def halo_coefs(s):
        def main(c, carry):
            q = c // per_q
            lanes = pl.ds(pl.multiple_of(lax.rem(c, per_q) * 128, 128), 128)
            for row, first, ok in ((8, 0, up_ok), (cy + 16, 16, down_ok)):
                label = ext[q, first : first + 16, lanes].astype(F32)[8 * s : 8 * s + 8]
                set_coefs(s, c, row, 8, only_if(ok, label, -1.0))
            return carry

        lax.fori_loop(0, tiles, main, 0)

        def get(side, slot):
            both = ext[n_il - 1 if side == 0 else 0, 32:48, 128 * slot : 128 * slot + 128].astype(F32)
            return both[8 * s : 8 * s + 8]

        edge_tiles(0, -1.0, get, lambda row, value: set_coefs(s, tiles, row, 8, value))

    def half_step(s, target, source, sign, last=False):
        rows = (size if last else size + 16) // 2
        lane = lane_ids(rows)
        for part in range(2):
            r = (16 if last else 8) + rows * part
            before, mid = source[tiles, r : r + rows, :], source[0, r : r + rows, :]
            for c in range(tiles if last else tiles + 1):
                after = source[(c + 1) % (tiles + 1), r : r + rows, :]
                vert = source[c, r - 1 : r - 1 + rows, :] + source[c, r + 1 : r + 1 + rows, :]
                left = pltpu.roll(jnp.where(lane == 127, before, mid), 1, 1)
                right = pltpu.roll(jnp.where(lane == 0, after, mid), 127, 1)
                total = vert + (left + right) + swing[s, c, r : r + rows, :] * mid
                target[c, r : r + rows, :] = (
                    damp[s, c, r : r + rows, :] * (
                        target[c, r : r + rows, :] + (RATE * RATE) * total if sign > 0 else target[c, r : r + rows, :] - total
                    )
                )
                before, mid = mid, after

    def transform(h):
        first = h * size

        def modulate(c, carry):
            lanes = pl.ds(pl.multiple_of(c * 128, 128), 128)
            cos = jnp.concatenate([turn[0, c]] * (size // 8))
            sin = jnp.concatenate([turn[1, c]] * (size // 8))
            real = fld[0][c, 16 : size + 16, :]
            imag = fld[1][c, 16 : size + 16, :] * (1.0 / RATE)
            out_stage[0, first : first + size, lanes] = real
            out_stage[1, first : first + size, lanes] = imag
            for n, value in enumerate((real * cos - imag * sin, real * sin + imag * cos)):
                high = value.astype(BF16)
                lhs[0, n * size : (n + 1) * size, lanes] = high
                lhs[1, n * size : (n + 1) * size, lanes] = (value - high.astype(F32)).astype(BF16)
            return carry

        lax.fori_loop(0, tiles, modulate, 0)
        pltpu.make_async_copy(
            out_stage.at[:, pl.ds(first, size), :], exit_ref.at[:, pl.ds(first, size), :], sem_out.at[h]
        ).start()
        lane = lane_ids(8)
        first_m = jnp.where((g == 0) | (g == n_gx - 1), 0, 1)
        for turn_no in range(det // 256):
            m = first_m + turn_no - 2 * first_m * turn_no
            cols = pl.ds(pl.multiple_of(256 * m, 256), 256)
            prod = jnp.dot(lhs[0], wx[0, :, cols], preferred_element_type=F32)
            prod += jnp.dot(lhs[1], wx[0, :, cols], preferred_element_type=F32)
            prod += jnp.dot(lhs[0], wx[1, :, cols], preferred_element_type=F32)
            c_re, s_re = prod[:size, :128], prod[:size, 128:]
            c_im, s_im = prod[size:, :128], prod[size:, 128:]
            rank = 128 * m + lane
            for block, freq, g_re, g_im in (
                (n_gx // 2 + m, rank, c_re + s_im, c_im - s_re),
                (n_gx // 2 - 1 - m, -rank - 1, c_re - s_im, c_im + s_re),
            ):
                quarter = lax.rem((freq + det) * g, n_gx) * (4 // n_gx)
                f_re = jnp.where(quarter == 0, 1.0, jnp.where(quarter == 2, -1.0, 0.0))
                f_im = jnp.where(quarter == 1, -1.0, jnp.where(quarter == 3, 1.0, 0.0))
                f_re = jnp.concatenate([f_re] * (size // 8))
                f_im = jnp.concatenate([f_im] * (size // 8))
                real, imag = g_re * f_re - g_im * f_im, g_re * f_im + g_im * f_re
                gown[block, 0:size, :] = real
                gown[block, size : 2 * size, :] = imag
                head, real, imag = encode(real, imag)
                gsend[block, h, 0:16, :] = head
                gsend[block, h, 16 : 16 + size, :] = real
                gsend[block, h, 16 + size : 16 + 2 * size, :] = imag
            opposite = add(g, 2, n_gx)
            if turn_no == 0:
                g_copy(h, 2).start()
                other = 2 * (n_gx // 2) - 1 - opposite
            else:
                other = 2 * (n_gx // 2) - 1 - g
            @pl.when(other != g)
            def _():
                g_copy(h, lax.rem(other - g + n_gx, n_gx)).start()

    def g_copy(h, d):
        block = add(g, d, n_gx)
        return remote(
            gsend.at[block, h], grecv.at[d - 1, h], g_send.at[h, d - 1], g_recv.at[h, d - 1], dev(gx=block)
        )

    def g_total(h):
        real, imag = gown[g, 0:size, :], gown[g, size : 2 * size, :]
        for d in range(1, n_gx):
            g_copy(h, d).wait_recv()
            more = decode(grecv[d - 1, h], size)
            real, imag = real + more[0], imag + more[1]
        return real, imag

    own_labels(0)
    pl.semaphore_wait(barrier, len(peers))
    send_own(0)
    own_labels(1)
    label_edges()
    for side, owner in ((0, 0), (1, n_il - 1)):
        @pl.when(i == owner)
        def _():
            for slot in range(3):
                lab_col_copy(side, slot).start()
    for side in range(2):
        go(edge_copy(side))
    for side in range(2):
        go(row_copy(side))
    load_fld.wait()
    for f in range(2):
        pack_fld[0, f] = pack_edge(stage[f, :, 0:128], False)
        pack_fld[1, f] = pack_edge(stage[f, :, cx - 128 : cx], True)
    for side in range(2):
        for slot in range(3):
            go(col_copy(side, slot))
    forward(0)
    for side in range(2):
        edge_copy(side).wait_recv()
    @pl.when((i == 0) | (i == n_il - 1))
    def _():
        for slot in range(3):
            lab_col_copy(0, slot).wait_recv()
        for d in range(1, n_il):
            ext_col_copy(d, i).start()
    for d in range(1, n_il):
        go(ext_copy(d))
    send_own(1)
    quarter_coefs(0, i)
    quarter_coefs(1, i)
    near(0)
    quarter_coefs(0, il_prev)
    quarter_coefs(0, il_next)
    for side in range(2):
        row_copy(side).wait_recv()
        for slot in range(3):
            col_copy(side, slot).wait_recv()
    assemble_field(0)
    arrived(0)
    quarter_coefs(0, il_far)
    for d in range(1, n_il):
        ext_copy(d).wait_recv()
    for owner in (0, n_il - 1):
        @pl.when(i != owner)
        def _():
            ext_col_copy(1, owner).wait_recv()
    halo_coefs(0)
    forward(1)
    for s in range(slices):
        for step in range(SUB):
            half_step(s, fld[0], fld[1], -1.0)
            half_step(s, fld[1], fld[0], 1.0, s == slices - 1 and step == SUB - 1)
        if s == 0:
            halo_coefs(1)
            near(1)
            quarter_coefs(1, il_prev)
            quarter_coefs(1, il_next)
            arrived(1)
            quarter_coefs(1, il_far)
    load_turn.wait()
    load_wx.wait()
    transform(0)

    load_ey.wait()
    for h in range(parts):
        for col, value in enumerate(g_total(h)):
            high = value.astype(BF16)
            low = (value - high.astype(F32)).astype(BF16)
            for n, piece in enumerate((high, low)):
                rhs[n, 0:cy, 128 * col : 128 * col + 128] = piece
                if col == 0:
                    rhs[n, cy : 2 * cy, 128:256] = -piece
                else:
                    rhs[n, cy : 2 * cy, 0:128] = piece

    share = det // n_gy
    half = det // 2
    odd = lax.rem(j, 2)

    def wave_rows(parity):
        rows = pl.ds(pl.multiple_of(parity * half, half), half)
        return (
            jnp.dot(ey[0, rows, :], rhs[0], preferred_element_type=F32)
            + jnp.dot(ey[1, rows, :], rhs[0], preferred_element_type=F32)
            + jnp.dot(ey[0, rows, :], rhs[1], preferred_element_type=F32)
        )

    def pair_copy(k):
        rows = pl.ds(k * half // 2, half // 2)
        return remote(
            fsend.at[rows, :], fpair.at[rows, :], pair_send.at[k], pair_recv.at[k], dev(gy=j + 1 - 2 * odd)
        )

    fsend[...] = wave_rows(1 - odd)
    for k in range(2):
        go(pair_copy(k))
    fhalf[...] = wave_rows(odd)
    for k in range(2):
        pair_copy(k).wait_recv()
    fhalf[...] += fpair[...]
    head, real, imag = encode(fhalf[:, 0:128], fhalf[:, 128:256])
    for k in range(n_gy // 2):
        rows = slice(k * share, (k + 1) * share)
        fcode[k, 0:16, :] = head
        fcode[k, 16 : 16 + share, :] = real[rows]
        fcode[k, 16 + share : 16 + 2 * share, :] = imag[rows]

    def f_copy(d):
        there = add(j, d, n_gy)
        return remote(
            fcode.at[there // 2], frecv.at[d // 2 - 1], f_send.at[d // 2 - 1], f_recv.at[d // 2 - 1], dev(gy=there)
        )

    order = sorted(range(2, n_gy, 2), key=lambda d: (abs(d - n_gy // 2), d))
    for d in order:
        go(f_copy(d))
    own = pl.ds(pl.multiple_of(j // 2 * share, share), share)
    acc = [fhalf[own, 0:128], fhalf[own, 128:256]]
    for d in order:
        f_copy(d).wait_recv()
        more = decode(frecv[d // 2 - 1], share)
        acc = [acc[0] + more[0], acc[1] + more[1]]
    row_id = lax.broadcasted_iota(jnp.int32, (128, 128), 0)
    col_id = lax.broadcasted_iota(jnp.int32, (128, 128), 1)
    mirror = jnp.full((128, 128), (g < n_gx // 2).astype(jnp.int32), jnp.int32)
    places = jnp.where(jnp.where(mirror > 0, 127 - col_id, col_id) == row_id, 1.0, 0.0)
    for n in range(2):
        far_ref[n] = jnp.dot(
            acc[n], places, precision=lax.Precision.HIGHEST, preferred_element_type=F32
        )

    for copy in pending:
        copy.wait_send()
    for n in range(len(chunks)):
        for way in range(2):
            for kind in range(3):
                chunk_copy(n, way, kind, i).wait_send()
    for h in range(parts):
        for d in range(1, n_gx):
            g_copy(h, d).wait_send()
    @pl.when((i == 0) | (i == n_il - 1))
    def _():
        for slot in range(3):
            lab_col_copy(0, slot).wait_send()
        for d in range(1, n_il):
            ext_col_copy(d, i).wait_send()
    for h in range(parts):
        rows = pl.ds(h * size, size)
        pltpu.make_async_copy(out_stage.at[:, rows, :], exit_ref.at[:, rows, :], sem_out.at[h]).wait()


def on_device(dims, det, incident, labels):
    n_il, n_gy, n_gx = dims
    slices, cy = labels.shape[:2]
    hbm_spec = pl.BlockSpec(memory_space=pltpu.HBM)
    qx = labels.shape[4]
    cx = incident.shape[3]
    ny, nx = cy * n_gy, cx * n_gx
    wave_x, turn, wave_y = tables(det, cy, cx, ny, nx)
    tiles = cx // 128
    size = cy // PARTS
    share = det // n_gy
    n_chunks = len(chunks_of(slices, cy, PARTS))
    dma = pltpu.SemaphoreType.DMA
    vmem = pltpu.VMEM
    any_spec = pl.BlockSpec(memory_space=pl.ANY)
    vmem_spec = pl.BlockSpec(memory_space=pltpu.VMEM)
    field, far = pl.pallas_call(
        functools.partial(kernel, dims),
        out_shape=(
            pltpu.VMEM((2, cy, cx), F32),
            pltpu.VMEM((2, share, 128), F32),
        ),
        in_specs=[hbm_spec] * 5,
        out_specs=(any_spec, vmem_spec),
        scratch_shapes=[
            vmem((slices * cy * qx // 128, 128), jnp.int32),
            vmem((2, cy, cx), F32),
            vmem((2, cy, cx), F32),
            vmem((n_il, slices, cy, qx), BF16),
            vmem((2, 8 * slices, qx), BF16),
            vmem((2, 8 * slices, 128), BF16),
            vmem((n_il, 24 * slices, qx), BF16),
            vmem((2, 2, 8, cx), F32),
            vmem((2, 2, 8, 128), F32),
            vmem((2, 3, 2, 8, 128), F32),
            vmem((tiles + 1, size + 32, 128), F32),
            vmem((tiles + 1, size + 32, 128), F32),
            vmem((slices, tiles + 1, size + 32, 128), F32),
            vmem((slices, tiles + 1, size + 32, 128), F32),
            vmem((2, tiles, 8, 128), F32),
            vmem((2, 2 * size, cx), BF16),
            vmem((2, cx, det), BF16),
            vmem((2, det, 2 * cy), BF16),
            vmem((n_gx, 2 * cy, 128), F32),
            vmem((n_gx, PARTS, 16 + 2 * size, 128), jnp.int16),
            vmem((n_gx - 1, PARTS, 16 + 2 * size, 128), jnp.int16),
            vmem((2, 2 * cy, 256), BF16),
            vmem((det // 2, 256), F32),
            vmem((det // 2, 256), F32),
            vmem((det // 2, 256), F32),
            vmem((n_gy // 2, 16 + 2 * share, 128), jnp.int16),
            vmem((n_gy // 2 - 1, 16 + 2 * share, 128), jnp.int16),
            dma((slices,)),
            dma((5,)),
            dma((PARTS,)),
            dma((n_chunks, 6)),
            dma((n_chunks, 6)),
            dma((2,)),
            dma((2,)),
            dma((3,)),
            dma((3,)),
            dma((n_il - 1,)),
            dma((n_il - 1,)),
            dma((n_il - 1,)),
            dma((2,)),
            dma((2,)),
            dma((2,)),
            dma((2, 3)),
            dma((2, 3)),
            dma((PARTS, n_gx - 1)),
            dma((PARTS, n_gx - 1)),
            dma((2,)),
            dma((2,)),
            dma((n_gy // 2 - 1,)),
            dma((n_gy // 2 - 1,)),
        ],
        compiler_params=pltpu.CompilerParams(
            collective_id=0, has_side_effects=True, vmem_limit_bytes=48 * 1024 * 1024
        ),
    )(
        *(
            pltpu.with_memory_space_constraint(x, pltpu.HBM)
            for x in (
                incident.reshape(2, cy, cx),
                labels.reshape(slices * cy * qx // 128, 128),
                jnp.asarray(wave_x),
                jnp.asarray(wave_y),
                jnp.asarray(turn),
            )
        )
    )
    return field[None], far[None]


def solution(mesh, det=DET):
    dims = tuple(mesh.shape[name] for name in ("illum", "gy", "gx"))
    in_specs = (P("illum", None, "gy", "gx"), P(None, "gy", "gx", "illum", None))
    out_specs = (P("illum", None, "gy", "gx"), P("illum", None, "gy", "gx"))
    return jax.shard_map(
        functools.partial(on_device, dims, det), mesh=mesh, in_specs=in_specs, out_specs=out_specs, check_vma=False
    )
```

```python
import functools
import math

import jax
import jax.numpy as jnp
import ml_dtypes
import numpy as np
from jax import lax
from jax.experimental import pallas as pl
from jax.experimental.pallas import tpu as pltpu
from jax.sharding import PartitionSpec as P

MESH = pl.DeviceIdType.MESH
SUB = 2
DET = 512
RATE = 0.24
PARTS = 1
F32 = jnp.float32
BF16 = jnp.bfloat16


def split(values):
    high = values.astype(ml_dtypes.bfloat16)
    low = (values - high.astype(np.float64)).astype(ml_dtypes.bfloat16)
    return np.stack([high, low])


def tables(det, cy, cx, ny, nx):
    cols = np.arange(cx)
    kappa = np.arange(det // 2) + 0.5
    angle = 2.0 * math.pi * cols[:, None] * kappa[None, :] / nx
    cos, sin = np.cos(angle), np.sin(angle)
    blocks = []
    for m in range(det // 256):
        blocks += [cos[:, 128 * m : 128 * m + 128], sin[:, 128 * m : 128 * m + 128]]
    wave_x = split(np.concatenate(blocks, axis=1))
    shift = math.pi * cols / nx
    turn = np.stack([np.cos(shift), np.sin(shift)]).astype(np.float32)
    turn = np.broadcast_to(turn.reshape(2, cx // 128, 1, 128), (2, cx // 128, 8, 128)).copy()
    share = det // (ny // cy)
    ky = (np.arange(det) - det // 2).reshape(-1, 2, share).transpose(1, 0, 2).reshape(-1)
    waves = []
    for tile in range(ny // cy):
        rows = tile * cy + np.arange(cy)
        angle = 2.0 * math.pi * ((ky[:, None] * rows[None, :]) % ny) / ny
        both = np.concatenate([np.cos(angle), np.sin(angle)], axis=1)
        waves.append(split(both / math.sqrt(ny * nx)))
    return wave_x, turn, np.stack(waves)


def lane_ids(rows):
    return lax.broadcasted_iota(jnp.int32, (rows, 128), 1)


def only_if(ok, value, other):
    flags = jnp.full(value.shape, ok.astype(jnp.int32), jnp.int32)
    return jnp.where(flags > 0, value, other)


def pack_edge(tiles, right):
    lane = lane_ids(8)
    out = jnp.zeros((8, 128), F32)
    for t in range(tiles.shape[0] // 8):
        piece = tiles[8 * t : 8 * t + 8]
        shift = (8 * t + (8 if right else 0)) % 128
        if shift:
            piece = pltpu.roll(piece, shift, 1)
        out = jnp.where(lane // 8 == t, piece, out)
    return out


def unpack_edges(left, right, t, fill, left_ok, right_ok):
    lane = lane_ids(8)
    shift_l, shift_r = (120 - 8 * t) % 128, (128 - 8 * t) % 128
    left = pltpu.roll(left, shift_l, 1) if shift_l else left
    right = pltpu.roll(right, shift_r, 1) if shift_r else right
    left = only_if(left_ok, left, fill)
    right = only_if(right_ok, right, fill)
    return jnp.where(lane < 8, right, jnp.where(lane >= 120, left, fill))


def coefficients(label):
    last = label > 6.5
    swing = jnp.where(last, 8.0, label) * (1.0 / (32.0 * RATE)) - 4.0
    loss = label + jnp.maximum(label - 4.0, 0.0) + jnp.where(last, 6.0, 0.0)
    damp = jnp.where(label < -0.5, 0.0, 1.0 - loss * (1.0 / 256.0))
    return swing, damp


def encode(real, imag):
    levels, bodies = [], []
    for value in (real, imag):
        top = jnp.maximum(jnp.max(jnp.abs(value), axis=0, keepdims=True), 2.0**-110)
        level = jnp.ceil(jnp.log2(top) * 128.0)
        levels.append(level)
        bodies.append(jnp.round(value * (jnp.exp2(level * (-1.0 / 128.0)) * 32000.0)).astype(jnp.int32).astype(jnp.int16))
    row = lax.broadcasted_iota(jnp.int32, (16, 128), 0)
    shape = (16, 128)
    head = jnp.where(row == 0, jnp.broadcast_to(levels[0], shape), jnp.broadcast_to(levels[1], shape))
    return head.astype(jnp.int32).astype(jnp.int16), bodies[0], bodies[1]


def decode(block, rows):
    unit = jnp.exp2(block[0:16].astype(jnp.int32).astype(F32) * (1.0 / 128.0)) * (1.0 / 32000.0)
    return [
        block[16 + n * rows : 16 + (n + 1) * rows].astype(jnp.int32).astype(F32) * unit[n : n + 1] for n in range(2)
    ]


def chunks_of(slices, cy, parts):
    if parts == 1:
        return [(s, 0, cy) for s in range(slices)]
    cut = cy // 2 + 16
    return [(s, a, b) for a, b in ((0, cut), (cut, cy)) for s in range(slices)]


def middle(n, a, b):
    step = (b - a) // 32 * 16
    return b - step if n % 2 else a + step


def kernel(
    dims, inc, lab, wx_hbm, ey_hbm, turn_hbm, exit_ref, far_ref,
    lab_in, stage, out_stage, labs, edge_src, pack_lab, ext, rowbuf, pack_fld, colbuf,
    fld_re, fld_im, swing, damp, turn, lhs, wx, ey, gown, gsend, grecv, rhs, fsend, fpair, fhalf, fcode, frecv,
    sem_lab, sem_in, sem_out, ag_send, ag_recv, edge_send, edge_recv, cl_send, cl_recv, ext_send, ext_recv, extc_send, extc_recv,
    row_send, row_recv, col_send, col_recv, g_send, g_recv, pair_send, pair_recv, f_send, f_recv,
):
    n_il, n_gy, n_gx = dims
    fld = (fld_re, fld_im)
    i, j, g = lax.axis_index("illum"), lax.axis_index("gy"), lax.axis_index("gx")
    _, slices, cy, qx = labs.shape
    cx = inc.shape[2]
    tiles = cx // 128
    per_q = qx // 128
    det = wx.shape[2]
    parts = PARTS
    size = cy // parts

    def dev(illum=None, gy=None, gx=None):
        return (
            i if illum is None else illum,
            j if gy is None else gy,
            g if gx is None else gx,
        )

    def add(value, step, count):
        return lax.rem(value + (step + count), count)

    def remote(src, dst, send, recv, target):
        return pltpu.make_async_remote_copy(
            src_ref=src, dst_ref=dst, send_sem=send, recv_sem=recv,
            device_id=target, device_id_type=MESH,
        )

    lab_rows = cy * per_q
    load_lab = [
        pltpu.make_async_copy(
            lab.at[pl.ds(s * lab_rows, lab_rows), :], lab_in.at[pl.ds(s * lab_rows, lab_rows), :], sem_lab.at[s]
        )
        for s in range(slices)
    ]
    load_fld = pltpu.make_async_copy(inc, stage, sem_in.at[1])
    load_wx = pltpu.make_async_copy(wx_hbm, wx, sem_in.at[2])
    load_ey = pltpu.make_async_copy(ey_hbm.at[j], ey, sem_in.at[3])
    load_turn = pltpu.make_async_copy(turn_hbm, turn, sem_in.at[4])
    for load in load_lab:
        load.start()
    load_fld.start()

    barrier = pltpu.get_barrier_semaphore()
    peers = [dev(illum=add(i, d, n_il)) for d in range(1, n_il)]
    peers += [
        dev(gy=add(j, dj, n_gy), gx=add(g, dg, n_gx))
        for dj in (-1, 0, 1) for dg in (-1, 0, 1) if dj or dg
    ]
    peers += [dev(gx=add(g, d, n_gx)) for d in range(2, n_gx - 1)]
    peers += [dev(gy=add(j, d, n_gy)) for d in range(2, n_gy, 2)]
    for peer in peers:
        pl.semaphore_signal(barrier, inc=1, device_id=peer, device_id_type=MESH)
    load_turn.start()
    load_wx.start()
    load_ey.start()

    def label_tile(s, row, rows, tile):
        return lab_in[pl.ds((s * cy + row) * per_q + tile, rows, stride=per_q), :].astype(F32)

    def own_labels(s):
        load_lab[s].wait()
        for tile in range(per_q):
            labs[i, s, :, 128 * tile : 128 * tile + 128] = label_tile(s, 0, cy, tile).astype(BF16)

    def label_edges():
        for e, top in ((0, 0), (1, cy - 8)):
            for tile in range(per_q):
                both = jnp.concatenate([label_tile(s, top, 8, tile) for s in range(slices)])
                edge_src[e, :, 128 * tile : 128 * tile + 128] = both.astype(BF16)
        for side, tile in ((0, 0), (1, per_q - 1)):
            both = jnp.concatenate([pack_edge(label_tile(s, 0, cy, tile), side == 1) for s in range(slices)])
            pack_lab[side] = both.astype(BF16)

    chunks = chunks_of(slices, cy, parts)
    il_next, il_prev = add(i, 1, n_il), add(i, -1, n_il)
    il_far = add(i, 2, n_il)

    def chunk_copy(n, way, kind, quarter):
        s, a, b = chunks[n]
        mid = middle(n, a, b)
        a, b = (a, mid) if (way == 0) == (kind != 1) else (mid, b)
        view = labs.at[quarter, s, pl.ds(a, b - a), :]
        slot = 3 * way + kind
        return remote(
            view, view, ag_send.at[n, slot], ag_recv.at[n, slot],
            dev(illum=il_next if way == 0 else il_prev),
        )

    pending = []

    def go(copy):
        copy.start()
        pending.append(copy)

    def start_chunk(copy):
        copy.start()

    def edge_copy(side):
        return remote(
            edge_src.at[side], ext.at[i, pl.ds(16 * (1 - side), 16), :], edge_send.at[side], edge_recv.at[side],
            dev(gy=add(j, 2 * side - 1, n_gy)),
        )

    def lab_col_copy(side, slot):
        return remote(
            pack_lab.at[side], ext.at[i, pl.ds(32, 16), pl.ds(128 * slot, 128)],
            cl_send.at[slot], cl_recv.at[slot], dev(gy=add(j, 1 - slot, n_gy), gx=add(g, 2 * side - 1, n_gx)),
        )

    def ext_copy(d):
        view = ext.at[i, pl.ds(0, 32), :]
        return remote(view, view, ext_send.at[d - 1], ext_recv.at[d - 1], dev(illum=add(i, d, n_il)))

    def ext_col_copy(d, source):
        view = ext.at[source, pl.ds(32, 16), pl.ds(0, 384)]
        return remote(
            view, view, extc_send.at[d - 1], extc_recv.at[lax.rem(source, 2)], dev(illum=add(i, d, n_il))
        )

    def row_copy(side):
        src = inc.at[:, pl.ds(0 if side == 0 else cy - 8, 8), :]
        return remote(
            src, rowbuf.at[1 - side], row_send.at[side], row_recv.at[side], dev(gy=add(j, 2 * side - 1, n_gy))
        )

    def col_copy(side, slot):
        return remote(
            pack_fld.at[side], colbuf.at[1 - side, slot], col_send.at[side, slot], col_recv.at[side, slot],
            dev(gy=add(j, 1 - slot, n_gy), gx=add(g, 2 * side - 1, n_gx)),
        )

    def send_own(n):
        for kind in range(2):
            for way in range(2):
                start_chunk(chunk_copy(n, way, kind, i))

    def forward(n):
        for way in range(2):
            src = il_prev if way == 0 else il_next
            chunk_copy(n, way, 0, src).wait_recv()
            start_chunk(chunk_copy(n, way, 2, src))

    def arrived(n):
        for way in range(2):
            chunk_copy(n, way, 2, il_far).wait_recv()

    def near(n):
        for way in range(2):
            chunk_copy(n, way, 1, il_prev if way == 0 else il_next).wait_recv()

    up_ok, down_ok = j > 0, j < n_gy - 1
    left_ok, right_ok = g > 0, g < n_gx - 1

    def assemble_field(h):
        first = h * size
        for f in range(2):
            rate = RATE if f else 1.0

            def main(c, carry):
                lanes = pl.ds(pl.multiple_of(c * 128, 128), 128)
                fld[f][c, 0:8, :] = jnp.zeros((8, 128), F32)
                fld[f][c, size + 24 : size + 32, :] = jnp.zeros((8, 128), F32)
                fld[f][c, 16 : size + 16, :] = stage[f, first : first + size, lanes] * rate
                if h == 0:
                    fld[f][c, 8:16, :] = only_if(up_ok, rowbuf[0, f, :, lanes], 0.0) * rate
                else:
                    fld[f][c, 8:16, :] = stage[f, first - 8 : first, lanes]
                if h == parts - 1:
                    fld[f][c, size + 16 : size + 24, :] = only_if(down_ok, rowbuf[1, f, :, lanes], 0.0) * rate
                else:
                    fld[f][c, size + 16 : size + 24, :] = stage[f, first + size : first + size + 8, lanes]
                return carry

            lax.fori_loop(0, tiles, main, 0)
            fld[f][tiles, 0:8, :] = jnp.zeros((8, 128), F32)
            fld[f][tiles, size + 24 : size + 32, :] = jnp.zeros((8, 128), F32)

        def put(f, row, value):
            fld[f][tiles, row : row + 8, :] = value

        for f in range(2):
            edge_tiles(
                h, 0.0, lambda side, slot: colbuf[side, slot, f], lambda row, value: put(f, row, value * (RATE if f else 1.0))
            )

    def edge_tiles(h, fill, get, put):
        total = cy // 8
        for t in range(h * size // 8 - 1, (h + 1) * size // 8 + 1):
            slot, rank, ok = (0, total - 1, up_ok) if t < 0 else (2, 0, down_ok) if t >= total else (1, t, None)
            both = (left_ok, right_ok) if ok is None else (left_ok & ok, right_ok & ok)
            value = unpack_edges(get(0, slot), get(1, slot), rank, fill, *both)
            put(16 + 8 * t - h * size, value)

    def set_coefs(s, c, row, rows, label):
        a, b = coefficients(label)
        swing[s, c, row : row + rows, :] = a
        damp[s, c, row : row + rows, :] = b

    def quarter_coefs(s, q):
        def main(tile, carry):
            lanes = pl.ds(pl.multiple_of(tile * 128, 128), 128)
            set_coefs(s, q * per_q + tile, 16, cy, labs[q, s, :, lanes].astype(F32))
            return carry

        lax.fori_loop(0, per_q, main, 0)

    def halo_coefs(s):
        def main(c, carry):
            q = c // per_q
            lanes = pl.ds(pl.multiple_of(lax.rem(c, per_q) * 128, 128), 128)
            for row, first, ok in ((8, 0, up_ok), (cy + 16, 16, down_ok)):
                label = ext[q, first : first + 16, lanes].astype(F32)[8 * s : 8 * s + 8]
                set_coefs(s, c, row, 8, only_if(ok, label, -1.0))
            return carry

        lax.fori_loop(0, tiles, main, 0)

        def get(side, slot):
            both = ext[n_il - 1 if side == 0 else 0, 32:48, 128 * slot : 128 * slot + 128].astype(F32)
            return both[8 * s : 8 * s + 8]

        edge_tiles(0, -1.0, get, lambda row, value: set_coefs(s, tiles, row, 8, value))

    def half_step(s, target, source, sign, last=False):
        rows = (size if last else size + 16) // 2
        lane = lane_ids(rows)
        for part in range(2):
            r = (16 if last else 8) + rows * part
            before, mid = source[tiles, r : r + rows, :], source[0, r : r + rows, :]
            for c in range(tiles if last else tiles + 1):
                after = source[(c + 1) % (tiles + 1), r : r + rows, :]
                vert = source[c, r - 1 : r - 1 + rows, :] + source[c, r + 1 : r + 1 + rows, :]
                left = pltpu.roll(jnp.where(lane == 127, before, mid), 1, 1)
                right = pltpu.roll(jnp.where(lane == 0, after, mid), 127, 1)
                total = vert + (left + right) + swing[s, c, r : r + rows, :] * mid
                target[c, r : r + rows, :] = (
                    damp[s, c, r : r + rows, :] * (
                        target[c, r : r + rows, :] + (RATE * RATE) * total if sign > 0 else target[c, r : r + rows, :] - total
                    )
                )
                before, mid = mid, after

    def transform(h):
        first = h * size

        def modulate(c, carry):
            lanes = pl.ds(pl.multiple_of(c * 128, 128), 128)
            cos = jnp.concatenate([turn[0, c]] * (size // 8))
            sin = jnp.concatenate([turn[1, c]] * (size // 8))
            real = fld[0][c, 16 : size + 16, :]
            imag = fld[1][c, 16 : size + 16, :] * (1.0 / RATE)
            out_stage[0, first : first + size, lanes] = real
            out_stage[1, first : first + size, lanes] = imag
            for n, value in enumerate((real * cos - imag * sin, real * sin + imag * cos)):
                high = value.astype(BF16)
                lhs[0, n * size : (n + 1) * size, lanes] = high
                lhs[1, n * size : (n + 1) * size, lanes] = (value - high.astype(F32)).astype(BF16)
            return carry

        lax.fori_loop(0, tiles, modulate, 0)
        pltpu.make_async_copy(
            out_stage.at[:, pl.ds(first, size), :], exit_ref.at[:, pl.ds(first, size), :], sem_out.at[h]
        ).start()
        lane = lane_ids(8)
        first_m = jnp.where((g == 0) | (g == n_gx - 1), 0, 1)
        for turn_no in range(det // 256):
            m = first_m + turn_no - 2 * first_m * turn_no
            cols = pl.ds(pl.multiple_of(256 * m, 256), 256)
            prod = jnp.dot(lhs[0], wx[0, :, cols], preferred_element_type=F32)
            prod += jnp.dot(lhs[1], wx[0, :, cols], preferred_element_type=F32)
            prod += jnp.dot(lhs[0], wx[1, :, cols], preferred_element_type=F32)
            c_re, s_re = prod[:size, :128], prod[:size, 128:]
            c_im, s_im = prod[size:, :128], prod[size:, 128:]
            rank = 128 * m + lane
            for block, freq, g_re, g_im in (
                (n_gx // 2 + m, rank, c_re + s_im, c_im - s_re),
                (n_gx // 2 - 1 - m, -rank - 1, c_re - s_im, c_im + s_re),
            ):
                quarter = lax.rem((freq + det) * g, n_gx) * (4 // n_gx)
                f_re = jnp.where(quarter == 0, 1.0, jnp.where(quarter == 2, -1.0, 0.0))
                f_im = jnp.where(quarter == 1, -1.0, jnp.where(quarter == 3, 1.0, 0.0))
                f_re = jnp.concatenate([f_re] * (size // 8))
                f_im = jnp.concatenate([f_im] * (size // 8))
                real, imag = g_re * f_re - g_im * f_im, g_re * f_im + g_im * f_re
                gown[block, 0:size, :] = real
                gown[block, size : 2 * size, :] = imag
                head, real, imag = encode(real, imag)
                gsend[block, h, 0:16, :] = head
                gsend[block, h, 16 : 16 + size, :] = real
                gsend[block, h, 16 + size : 16 + 2 * size, :] = imag
            opposite = add(g, 2, n_gx)
            if turn_no == 0:
                g_copy(h, 2).start()
                other = 2 * (n_gx // 2) - 1 - opposite
            else:
                other = 2 * (n_gx // 2) - 1 - g
            @pl.when(other != g)
            def _():
                g_copy(h, lax.rem(other - g + n_gx, n_gx)).start()

    def g_copy(h, d):
        block = add(g, d, n_gx)
        return remote(
            gsend.at[block, h], grecv.at[d - 1, h], g_send.at[h, d - 1], g_recv.at[h, d - 1], dev(gx=block)
        )

    def g_total(h):
        real, imag = gown[g, 0:size, :], gown[g, size : 2 * size, :]
        for d in range(1, n_gx):
            g_copy(h, d).wait_recv()
            more = decode(grecv[d - 1, h], size)
            real, imag = real + more[0], imag + more[1]
        return real, imag

    own_labels(0)
    pl.semaphore_wait(barrier, len(peers))
    send_own(0)
    own_labels(1)
    label_edges()
    for side, owner in ((0, 0), (1, n_il - 1)):
        @pl.when(i == owner)
        def _():
            for slot in range(3):
                lab_col_copy(side, slot).start()
    for side in range(2):
        go(edge_copy(side))
    for side in range(2):
        go(row_copy(side))
    load_fld.wait()
    for f in range(2):
        pack_fld[0, f] = pack_edge(stage[f, :, 0:128], False)
        pack_fld[1, f] = pack_edge(stage[f, :, cx - 128 : cx], True)
    for side in range(2):
        for slot in range(3):
            go(col_copy(side, slot))
    forward(0)
    for side in range(2):
        edge_copy(side).wait_recv()
    @pl.when((i == 0) | (i == n_il - 1))
    def _():
        for slot in range(3):
            lab_col_copy(0, slot).wait_recv()
        for d in range(1, n_il):
            ext_col_copy(d, i).start()
    for d in range(1, n_il):
        go(ext_copy(d))
    send_own(1)
    quarter_coefs(0, i)
    quarter_coefs(1, i)
    near(0)
    quarter_coefs(0, il_prev)
    quarter_coefs(0, il_next)
    for side in range(2):
        row_copy(side).wait_recv()
        for slot in range(3):
            col_copy(side, slot).wait_recv()
    assemble_field(0)
    arrived(0)
    quarter_coefs(0, il_far)
    for d in range(1, n_il):
        ext_copy(d).wait_recv()
    for owner in (0, n_il - 1):
        @pl.when(i != owner)
        def _():
            ext_col_copy(1, owner).wait_recv()
    halo_coefs(0)
    forward(1)
    for s in range(slices):
        for step in range(SUB):
            half_step(s, fld[0], fld[1], -1.0)
            half_step(s, fld[1], fld[0], 1.0, s == slices - 1 and step == SUB - 1)
        if s == 0:
            halo_coefs(1)
            near(1)
            quarter_coefs(1, il_prev)
            quarter_coefs(1, il_next)
            arrived(1)
            quarter_coefs(1, il_far)
    load_turn.wait()
    load_wx.wait()
    transform(0)

    load_ey.wait()
    for h in range(parts):
        for col, value in enumerate(g_total(h)):
            high = value.astype(BF16)
            low = (value - high.astype(F32)).astype(BF16)
            for n, piece in enumerate((high, low)):
                rhs[n, 0:cy, 128 * col : 128 * col + 128] = piece
                if col == 0:
                    rhs[n, cy : 2 * cy, 128:256] = -piece
                else:
                    rhs[n, cy : 2 * cy, 0:128] = piece

    share = det // n_gy
    half = det // 2
    odd = lax.rem(j, 2)

    def wave_rows(parity):
        rows = pl.ds(pl.multiple_of(parity * half, half), half)
        return (
            jnp.dot(ey[0, rows, :], rhs[0], preferred_element_type=F32)
            + jnp.dot(ey[1, rows, :], rhs[0], preferred_element_type=F32)
            + jnp.dot(ey[0, rows, :], rhs[1], preferred_element_type=F32)
        )

    def pair_copy(k):
        rows = pl.ds(k * half // 2, half // 2)
        return remote(
            fsend.at[rows, :], fpair.at[rows, :], pair_send.at[k], pair_recv.at[k], dev(gy=j + 1 - 2 * odd)
        )

    fsend[...] = wave_rows(1 - odd)
    for k in range(2):
        go(pair_copy(k))
    fhalf[...] = wave_rows(odd)
    for k in range(2):
        pair_copy(k).wait_recv()
    fhalf[...] += fpair[...]
    head, real, imag = encode(fhalf[:, 0:128], fhalf[:, 128:256])
    for k in range(n_gy // 2):
        rows = slice(k * share, (k + 1) * share)
        fcode[k, 0:16, :] = head
        fcode[k, 16 : 16 + share, :] = real[rows]
        fcode[k, 16 + share : 16 + 2 * share, :] = imag[rows]

    def f_copy(d):
        there = add(j, d, n_gy)
        return remote(
            fcode.at[there // 2], frecv.at[d // 2 - 1], f_send.at[d // 2 - 1], f_recv.at[d // 2 - 1], dev(gy=there)
        )

    order = sorted(range(2, n_gy, 2), key=lambda d: (abs(d - n_gy // 2), d))
    for d in order:
        go(f_copy(d))
    own = pl.ds(pl.multiple_of(j // 2 * share, share), share)
    acc = [fhalf[own, 0:128], fhalf[own, 128:256]]
    for d in order:
        f_copy(d).wait_recv()
        more = decode(frecv[d // 2 - 1], share)
        acc = [acc[0] + more[0], acc[1] + more[1]]
    row_id = lax.broadcasted_iota(jnp.int32, (128, 128), 0)
    col_id = lax.broadcasted_iota(jnp.int32, (128, 128), 1)
    mirror = jnp.full((128, 128), (g < n_gx // 2).astype(jnp.int32), jnp.int32)
    places = jnp.where(jnp.where(mirror > 0, 127 - col_id, col_id) == row_id, 1.0, 0.0)
    for n in range(2):
        far_ref[n] = jnp.dot(
            acc[n], places, precision=lax.Precision.HIGHEST, preferred_element_type=F32
        )

    for copy in pending:
        copy.wait_send()
    for n in range(len(chunks)):
        for way in range(2):
            for kind in range(3):
                chunk_copy(n, way, kind, i).wait_send()
    for h in range(parts):
        for d in range(1, n_gx):
            g_copy(h, d).wait_send()
    @pl.when((i == 0) | (i == n_il - 1))
    def _():
        for slot in range(3):
            lab_col_copy(0, slot).wait_send()
        for d in range(1, n_il):
            ext_col_copy(d, i).wait_send()
    for h in range(parts):
        rows = pl.ds(h * size, size)
        pltpu.make_async_copy(out_stage.at[:, rows, :], exit_ref.at[:, rows, :], sem_out.at[h]).wait()


def on_device(dims, det, incident, labels):
    n_il, n_gy, n_gx = dims
    slices, cy = labels.shape[:2]
    hbm_spec = pl.BlockSpec(memory_space=pltpu.HBM)
    qx = labels.shape[4]
    cx = incident.shape[3]
    ny, nx = cy * n_gy, cx * n_gx
    wave_x, turn, wave_y = tables(det, cy, cx, ny, nx)
    tiles = cx // 128
    size = cy // PARTS
    share = det // n_gy
    n_chunks = len(chunks_of(slices, cy, PARTS))
    dma = pltpu.SemaphoreType.DMA
    vmem = pltpu.VMEM
    any_spec = pl.BlockSpec(memory_space=pl.ANY)
    vmem_spec = pl.BlockSpec(memory_space=pltpu.VMEM)
    field, far = pl.pallas_call(
        functools.partial(kernel, dims),
        out_shape=(
            pltpu.VMEM((2, cy, cx), F32),
            pltpu.VMEM((2, share, 128), F32),
        ),
        in_specs=[hbm_spec] * 5,
        out_specs=(any_spec, vmem_spec),
        scratch_shapes=[
            vmem((slices * cy * qx // 128 + 8, 128), jnp.int32),
            vmem((2, cy, cx), F32),
            vmem((2, cy, cx), F32),
            vmem((n_il, slices, cy, qx), BF16),
            vmem((2, 8 * slices, qx), BF16),
            vmem((2, 8 * slices, 128), BF16),
            vmem((n_il, 24 * slices, qx), BF16),
            vmem((2, 2, 8, cx), F32),
            vmem((2, 2, 8, 128), F32),
            vmem((2, 3, 2, 8, 128), F32),
            vmem((tiles + 1, size + 32, 128), F32),
            vmem((tiles + 1, size + 32, 128), F32),
            vmem((slices, tiles + 1, size + 32, 128), F32),
            vmem((slices, tiles + 1, size + 32, 128), F32),
            vmem((2, tiles, 8, 128), F32),
            vmem((2, 2 * size, cx), BF16),
            vmem((2, cx, det), BF16),
            vmem((2, det, 2 * cy), BF16),
            vmem((n_gx, 2 * cy, 128), F32),
            vmem((n_gx, PARTS, 16 + 2 * size, 128), jnp.int16),
            vmem((n_gx - 1, PARTS, 16 + 2 * size, 128), jnp.int16),
            vmem((2, 2 * cy, 256), BF16),
            vmem((det // 2, 256), F32),
            vmem((det // 2, 256), F32),
            vmem((det // 2, 256), F32),
            vmem((n_gy // 2, 16 + 2 * share, 128), jnp.int16),
            vmem((n_gy // 2 - 1, 16 + 2 * share, 128), jnp.int16),
            dma((slices,)),
            dma((5,)),
            dma((PARTS,)),
            dma((n_chunks, 6)),
            dma((n_chunks, 6)),
            dma((2,)),
            dma((2,)),
            dma((3,)),
            dma((3,)),
            dma((n_il - 1,)),
            dma((n_il - 1,)),
            dma((n_il - 1,)),
            dma((2,)),
            dma((2,)),
            dma((2,)),
            dma((2, 3)),
            dma((2, 3)),
            dma((PARTS, n_gx - 1)),
            dma((PARTS, n_gx - 1)),
            dma((2,)),
            dma((2,)),
            dma((n_gy // 2 - 1,)),
            dma((n_gy // 2 - 1,)),
        ],
        compiler_params=pltpu.CompilerParams(
            collective_id=0, has_side_effects=True, vmem_limit_bytes=48 * 1024 * 1024
        ),
    )(
        *(
            pltpu.with_memory_space_constraint(x, pltpu.HBM)
            for x in (
                incident.reshape(2, cy, cx),
                labels.reshape(slices * cy * qx // 128, 128),
                jnp.asarray(wave_x),
                jnp.asarray(wave_y),
                jnp.asarray(turn),
            )
        )
    )
    return field[None], far[None]


def solution(mesh, det=DET):
    dims = tuple(mesh.shape[name] for name in ("illum", "gy", "gx"))
    in_specs = (P("illum", None, "gy", "gx"), P(None, "gy", "gx", "illum", None))
    out_specs = (P("illum", None, "gy", "gx"), P("illum", None, "gy", "gx"))
    return jax.shard_map(
        functools.partial(on_device, dims, det), mesh=mesh, in_specs=in_specs, out_specs=out_specs, check_vma=False
    )
```
